32 devices in a mesh: grp: 2 (over y), span: 4 (over z), stream: 2 (over x), vert: 2 (over core).
Axes of the slice: x: 2, y: 2, z: 4, core: 2. Of those that a mesh axis runs over, the one named last changes fastest.
Arguments:
- kappa: float32 [64, 64, 512], P(('grp', 'stream'), 'span', 'vert'), parts along dimension 0, may hold values from 0.01 to 0.16
- sigma: float32 [64, 64, 512], P(('grp', 'stream'), 'span', 'vert'), parts along dimension 0, may hold values from 0.5 to 2
- gate_residual: float32 [4, 2, 4096], P(('grp', 'stream'), 'vert', 'span'), parts along dimension 0, may hold values from -6 to 6
- gate_azimuth: float32 [4, 2, 4096], P(('grp', 'stream'), 'vert', 'span'), parts along dimension 0, may hold values from -3.140625 to 3.140625
- gate_elevation: float32 [4, 2, 4096], P(('grp', 'stream'), 'vert', 'span'), parts along dimension 0, may hold values from -0.3 to 0.3
- gate_brick: int32 [4, 2, 4096, 1], P(('grp', 'stream'), 'vert', 'span'), parts along dimension 0, may hold values from 0 to 3; in each aligned block of 1024 rows (0 to 1023, 1024 to 2047, ..., all dimensions but the last counted through in order) at most 768 rows name the same one
- gate_cell: int32 [4, 2, 4096], P(('grp', 'stream'), 'vert', 'span'), parts along dimension 0, may hold values from 0 to 65535
- blade_force: float32 [3, 4, 1024], P(None, ('grp', 'stream'), 'span'), parts along dimension 1, may hold values from -6 to 6
- point_x: float32 [4, 1024], P(('grp', 'stream'), 'span'), parts along dimension 0, may hold values from 6 to 9
- point_y: float32 [4, 1024], P(('grp', 'stream'), 'span'), parts along dimension 0, may hold values from 0 to 16
- point_z: float32 [4, 1024], P(('grp', 'stream'), 'span'), parts along dimension 0, may hold values from 0 to 512
Outputs:
- increment: float32 [3, 64, 64, 512], P(None, ('grp', 'stream'), 'span', 'vert'), parts along dimension 1
The draws below stay inside these ranges and needn't reach their ends.
There are 2 independent parts, one for each index of `grp`. The reference program is written for one: setup_inputs(seed, part) draws one part's arguments, and reference() takes and returns one part's arrays. A program takes and returns all parts, laid end to end along the dimension named above; each array names one. Nothing has to cross between parts.
Inputs may be any that keep to these rules, and one draw needn't show every extreme that they name: `gate_brick`: among the 1024 gate rows of one brick (aligned blocks of rows), at most 768 name one spanwise brick, and in every draw some brick is named by exactly 768 of them.
All inputs are finite; a program needn't handle non-finite values.
Results may differ from the reference program's by a relative error of at most 0.0003.
Values sent between devices are 32-bit elements; how exact they have to be, the bound alone decides.
No kernel may reach another device: no remote copies, remote signals or barrier semaphores. Data moves between devices by JAX's collectives and lax.ppermute only.
A program may use at most 128 MiB of HBM per device.

```python
import math
import jax
import jax.numpy as jnp
import numpy as np
from jax import lax

CX = 16
CY = 16
CZ = 256
GATE_DEV = 1024
PTS = 256
SPREAD = 6
PASSES = 4
NX = 32
NY = 64
NZ = 512
BANDS = 2
HALVES = 2
GATES = 4096
POINTS = 1024
CAP = 768
CELLS = 65536
N_SPAN = 4


def set_ends(result, own_key, smallest, high):
    extent = result.shape
    spot = [jax.random.randint(jax.random.fold_in(own_key, axis), (), 0, extent[axis]) for axis in range(len(extent))]
    result = result.at[tuple(spot)].set(smallest)
    longest = extent.index(max(extent))
    spot[longest] = (spot[longest] + 1) % extent[longest]
    return result.at[tuple(spot)].set(high)


def shard_levels(rng, dims, split, smallest, largest):
    def one(dim, blocks):
        draws = jax.random.uniform(jax.random.fold_in(jax.random.fold_in(rng, 6), dim), (blocks,), jnp.float32, smallest / len(split), largest / len(split))
        return jnp.repeat(jnp.exp(draws), dims[dim] // blocks).reshape((-1,) + (1,) * (len(dims) - dim - 1))

    gain = one(*split[0])
    for cut in split[1:]:
        gain = gain * one(*cut)
    return gain


def shared_out(own_key, own, number, rows, count, top, limit, slope):
    order = jax.random.permutation(own_key, count)
    packed, usual = portions_of(count, rows * top, limit, slope, True), portions_of(count, rows * top, limit, slope, False)
    places = jnp.arange(count)

    def named(lengths, rotation):
        used = int((lengths > 0).sum())
        fixed = max(1, used // 4)
        moved = fixed + (places - fixed + rotation * (used - fixed)) % max(1, count - fixed)
        return jnp.zeros((count,), jnp.int32).at[order[jnp.where(places < fixed, places, moved)]].set(jnp.asarray(lengths, jnp.int32))

    lengths = jnp.where(number % 4 == 0, named(packed, number // 4), named(usual, number - number // 4 - 1))
    mixed = jax.random.permutation(jax.random.fold_in(own, 3), count)
    source_of, receiver = mixed[0:count // 2 * 2:2], mixed[1:count // 2 * 2:2]
    slack = jnp.minimum(lengths[source_of] - 1, limit - lengths[receiver]) // 2
    slack = jnp.where((source_of == order[0]) | (receiver == order[0]) | (lengths[receiver] == 0), 0, jnp.maximum(slack, 0))
    moved = jax.random.randint(jax.random.fold_in(own, 4), (count // 2,), 0, 1 << 20) % (slack + 1)
    lengths = lengths.at[source_of].add(-moved).at[receiver].add(moved)
    items = jnp.searchsorted(jnp.cumsum(lengths), jnp.arange(rows * top), side="right").astype(jnp.int32)
    table = items.reshape(top, rows).T
    table = table[jax.random.permutation(jax.random.fold_in(own, 1), rows)]
    rotation = jax.random.randint(jax.random.fold_in(own, 2), (rows, 1), 0, top)
    return jnp.take_along_axis(table, (jnp.arange(top)[None, :] + rotation) % top, axis=1)


def portions_of(amount, total, limit, lean, full):
    loads = [(1 << 20) // math.isqrt(rank ** lean) + 1 for rank in range(1, amount + 1)]
    largest = limit if full else min(limit, max(-(-total // amount), total * loads[0] // sum(loads)))
    least = 1 if total - largest >= amount - 1 else 0
    given, surplus = [largest] + [least] * (amount - 1), total - largest - least * (amount - 1)
    while surplus > 0:
        free = [i for i in range(1, amount) if given[i] < largest] or [i for i in range(1, amount) if given[i] < limit]
        mass, budget = sum([loads[i] for i in free]), surplus
        for i in free:
            more = min(limit - given[i], max(1, budget * loads[i] // mass), surplus)
            given[i] = given[i] + more
            surplus = surplus - more
    return np.array(given)


def centred(rng, extent, scale, bound, cuts=(), kind=jnp.bfloat16):
    entries = jax.random.normal(rng, extent, jnp.float32) * scale
    if len(cuts) > 0:
        entries = shard_levels(rng, extent, cuts, -0.22, 0.18) * entries
    return jnp.clip(entries, min=-bound, max=bound).astype(kind)


def setup_inputs(seed: int = 0, part: int = 0) -> dict:
    key_list = jax.random.split(jax.random.key(seed), 12)
    part_keys = jax.random.split(jax.random.fold_in(key_list[11], part), 12)
    kappa = jnp.clip(jnp.exp(math.log(0.16) - 2.7725887 * jax.random.uniform(part_keys[0], (NX, NY, NZ), jnp.float32) ** shard_levels(part_keys[0], (NX, NY, NZ), ((0, 2), (1, 4), (2, 2)), -0.2, 0.2)), 0.01, 0.16)
    sigma = jnp.clip(jnp.exp(math.log(2.0) - 1.3862944 * jax.random.uniform(part_keys[1], (NX, NY, NZ), jnp.float32) ** shard_levels(part_keys[1], (NX, NY, NZ), ((0, 2), (1, 4), (2, 2)), -0.2, 0.2)), 0.5, 2.0)
    gate_residual = centred(part_keys[2], (BANDS, HALVES, GATES), 1.0, 6.0, ((0, 2), (1, 2), (2, 4)), jnp.float32)
    gate_azimuth = jnp.clip(jax.random.uniform(part_keys[3], (BANDS, HALVES, GATES), jnp.float32, -3.140625, 3.140625), -3.140625, 3.140625)
    gate_elevation = jnp.clip(jax.random.uniform(part_keys[4], (BANDS, HALVES, GATES), jnp.float32, -0.3, 0.3) * shard_levels(part_keys[4], (BANDS, HALVES, GATES), ((0, 2), (1, 2), (2, 4)), -0.4, 0.0), -0.3, 0.3)
    gate_brick_keys = jax.random.split(jax.random.fold_in(part_keys[5], 1), BANDS * HALVES * GATES // GATE_DEV)
    gate_brick_turns = jax.random.permutation(jax.random.fold_in(part_keys[5], 3), BANDS * HALVES * GATES // GATE_DEV)
    gate_brick = jax.vmap(lambda own, number: shared_out(jax.random.fold_in(part_keys[5], 2), own, number, GATE_DEV, N_SPAN, 1, CAP, 2))(gate_brick_keys, gate_brick_turns).reshape((BANDS, HALVES, GATES, 1))
    gate_cell = set_ends(jax.random.randint(part_keys[6], (BANDS, HALVES, GATES), 0, CELLS), jax.random.fold_in(part_keys[6], 1), 0, CELLS - 1).astype(jnp.int32)
    blade_force = centred(part_keys[7], (3, BANDS, POINTS), 1.0, 6.0, ((1, 2), (2, 4)), jnp.float32)
    point_x = jnp.clip(6.0 + 3.0 * jax.random.uniform(part_keys[8], (BANDS, POINTS), jnp.float32) ** shard_levels(part_keys[8], (BANDS, POINTS), ((0, 2), (1, 4)), -0.2, 0.2), 6.0, 9.0)
    point_y = jnp.clip(16.0 * jax.random.uniform(part_keys[9], (BANDS, POINTS), jnp.float32) ** shard_levels(part_keys[9], (BANDS, POINTS), ((0, 2), (1, 4)), -0.2, 0.2), 0.0, 16.0)
    point_z = jnp.clip(512.0 * jax.random.uniform(part_keys[10], (BANDS, POINTS), jnp.float32) ** shard_levels(part_keys[10], (BANDS, POINTS), ((0, 2), (1, 4)), -0.2, 0.2), 0.0, 512.0)
    return {"kappa": kappa, "sigma": sigma, "gate_residual": gate_residual, "gate_azimuth": gate_azimuth, "gate_elevation": gate_elevation, "gate_brick": gate_brick, "gate_cell": gate_cell, "blade_force": blade_force, "point_x": point_x, "point_y": point_y, "point_z": point_z}


def bump(distance, reach):
    scaled = distance / reach
    return jnp.square(jnp.maximum(0.0, 1.0 - scaled * scaled))

def lidar_part(gate_residual, gate_azimuth, gate_elevation, gate_brick, gate_cell):
    cosine = jnp.cos(gate_elevation)
    weighted = jnp.stack([cosine * jnp.cos(gate_azimuth), cosine * jnp.sin(gate_azimuth), jnp.sin(gate_elevation)]) * gate_residual[None]
    band_index = lax.broadcasted_iota(jnp.int32, gate_cell.shape, 0)
    layer_index = lax.broadcasted_iota(jnp.int32, gate_cell.shape, 1)
    brick_index = gate_brick[..., 0]
    coord_x = band_index * CX + gate_cell // (CY * CZ)
    coord_y = brick_index * CY + gate_cell // CZ % CY
    coord_z = layer_index * CZ + gate_cell % CZ
    field = jnp.zeros((3, NX, NY, NZ), jnp.float32)
    return field.at[:, coord_x.reshape(-1), coord_y.reshape(-1), coord_z.reshape(-1)].add(weighted.reshape(3, -1))

def rotor_part(blade_force, point_x, point_y, point_z):
    reach = jnp.float32(SPREAD)
    x_cells = jnp.arange(CX, dtype=jnp.float32)
    y_cells = jnp.arange(CY, dtype=jnp.float32)
    z_cells = jnp.arange(NZ, dtype=jnp.float32)
    zero_index = jnp.int32(0)

    def one_brick(brick_number):
        band = (brick_number // N_SPAN).astype(jnp.int32)
        column = (brick_number % N_SPAN).astype(jnp.int32)
        forces = []
        x_parts = []
        y_parts = []
        z_parts = []
        for side_offset in (-1, 0, 1):
            owner = ((column + side_offset) % N_SPAN).astype(jnp.int32)
            start = (owner * PTS).astype(jnp.int32)
            forces.append(lax.dynamic_slice(blade_force, (zero_index, band, start), (3, 1, PTS))[:, 0])
            x_parts.append(lax.dynamic_slice(point_x, (band, start), (1, PTS))[0])
            y_here = lax.dynamic_slice(point_y, (band, start), (1, PTS))[0]
            shifted = y_cells - jnp.float32(side_offset * CY)
            y_parts.append(bump(shifted[:, None] - y_here[None, :], reach))
            z_parts.append(lax.dynamic_slice(point_z, (band, start), (1, PTS))[0])
        force_all = jnp.concatenate(forces, axis=1)
        kernel_x = bump(x_cells[:, None] - jnp.concatenate(x_parts)[None, :], reach)
        kernel_y = jnp.concatenate(y_parts, axis=1)
        kernel_z = bump(z_cells[:, None] - jnp.concatenate(z_parts)[None, :], reach)
        blocks = []
        for component in range(3):
            weights = (force_all[component][None, None, :] * kernel_x[:, None, :] * kernel_y[None, :, :]).reshape(CX * CY, 3 * PTS)
            blocks.append(jnp.dot(weights, kernel_z.T, precision=lax.Precision.HIGHEST).reshape(CX, CY, NZ))
        return jnp.stack(blocks)
    bricks = lax.map(one_brick, jnp.arange(BANDS * N_SPAN, dtype=jnp.int32))
    bricks = bricks.reshape(BANDS, N_SPAN, 3, CX, CY, NZ).transpose(2, 0, 3, 1, 4, 5)
    return bricks.reshape(3, NX, NY, NZ)

def diffuse(values, along_x, along_y, along_z):
    flux_x = along_x * (values[1:] - values[:-1])
    flux_y = along_y * (jnp.roll(values, -1, 1) - values)
    flux_z = along_z * (values[:, :, 1:] - values[:, :, :-1])
    change = jnp.pad(flux_x, ((0, 1), (0, 0), (0, 0))) - jnp.pad(flux_x, ((1, 0), (0, 0), (0, 0)))
    change = change + (flux_y - jnp.roll(flux_y, 1, 1))
    change = change + (jnp.pad(flux_z, ((0, 0), (0, 0), (0, 1))) - jnp.pad(flux_z, ((0, 0), (0, 0), (1, 0))))
    return values + change

def reference(kappa, sigma, gate_residual, gate_azimuth, gate_elevation, gate_brick, gate_cell, blade_force, point_x, point_y, point_z):
    lidar = lidar_part(gate_residual, gate_azimuth, gate_elevation, gate_brick, gate_cell)
    rotor = rotor_part(blade_force, point_x, point_y, point_z)
    source = (lidar + rotor) * sigma[None]
    along_x = jnp.sqrt(kappa[:-1] * kappa[1:])
    along_y = jnp.sqrt(kappa * jnp.roll(kappa, -1, 1))
    along_z = jnp.sqrt(kappa[:, :, :-1] * kappa[:, :, 1:])

    def one_component(values):
        for pass_index in range(PASSES):
            values = diffuse(values, along_x, along_y, along_z)
        return values
    return lax.map(one_component, source)
```

```python
import functools

import jax
import jax.numpy as jnp
from jax import lax
from jax.experimental import pallas as pl
from jax.experimental.pallas import tpu as pltpu
from jax.sharding import PartitionSpec as P

SPREAD = 6
PASSES = 4
HALO = 4
BF16 = jnp.bfloat16
F32 = jnp.float32
CONTRACT_LANES = (((1,), (1,)), ((), ()))


def bump(distance):
    scaled = distance * F32(1.0 / SPREAD)
    return jnp.square(jnp.maximum(0.0, 1.0 - scaled * scaled))


def two_parts(values):
    high = values.astype(BF16)
    return high, (values - high.astype(F32)).astype(BF16)


def dot_lanes(left, right):
    return lax.dot_general(left, right, CONTRACT_LANES, preferred_element_type=F32)


def pack_kernel(sides, res, azi, ele, brick, cell, force, px, py, pz, kappa, sigma, payload, *slabs):
    size_x = kappa.shape[0]
    cosine = jnp.cos(ele[0])
    value = res[0]
    payload[0:1, :] = cosine * jnp.cos(azi[0]) * value
    payload[1:2, :] = cosine * jnp.sin(azi[0]) * value
    payload[2:3, :] = jnp.sin(ele[0]) * value
    payload[3:4, :] = brick[...].astype(F32)
    payload[4:5, :] = cell[0].astype(F32)
    points = px.shape[1]
    payload[5:8, :] = jnp.zeros((3, payload.shape[1]), F32)
    for c in range(3):
        payload[5:6, c * points : (c + 1) * points] = force[c]
    payload[5:6, 3 * points : 4 * points] = px[...]
    payload[6:7, 0:points] = py[...]
    payload[6:7, points : 2 * points] = pz[...]
    if sides == 1:
        starts = [jnp.where(lax.axis_index("stream") == 0, size_x - HALO, 0)]
    else:
        starts = [size_x - HALO, 0]
    for slab, start in zip(slabs, starts):
        slab[0] = kappa[pl.ds(start, HALO)]
        slab[1] = sigma[pl.ds(start, HALO)]


def sort_kernel(spans, sides, count, *refs):
    payloads, (kappa, sigma), slabs, (rows, to_upper, to_lower) = (
        refs[:count],
        refs[count : count + 2],
        refs[count + 2 : count + 2 + sides],
        refs[count + 2 + sides :],
    )
    size_x, size_y, size_z = kappa.shape
    ext_y = size_y + 2 * HALO
    me = lax.axis_index("span")

    def payload_of(j):
        return payloads[j] if count > 1 else payloads[0].at[j]

    for j in range(spans):
        one = payload_of(j)
        brick = one[3:4, :].astype(jnp.int32)
        cell = one[4:5, :].astype(jnp.int32)
        away = brick - me
        away = jnp.where(away < 0, away + spans, away)
        x = cell // (size_y * size_z)
        y = cell // size_z % size_y
        z = cell % size_z
        row = jnp.where(
            away == 0,
            y,
            jnp.where(
                (away == 1) & (y < HALO),
                y + size_y,
                jnp.where((away == spans - 1) & (y >= size_y - HALO), y + 2 * HALO, -1),
            ),
        )
        place = jnp.where(row < 0, -1, (x * ext_y + row) * size_z + z)
        rows[j, 0:3, :] = one[0:3, :]
        rows[j, 3:4, :] = place.astype(F32)
    points = rows.shape[2] // 4
    rows[spans] = jnp.zeros(rows.shape[1:], F32)
    rows[spans + 1] = jnp.zeros(rows.shape[1:], F32)
    near = (0, 1, 2) if count > 1 else (0, spans - 1, 1)
    for k, (j, offset) in enumerate(zip(near, (0, -1, 1))):
        one = payload_of(j)
        lanes = slice(k * points, (k + 1) * points)
        for c in range(4):
            rows[spans, c : c + 1, lanes] = one[5:6, c * points : (c + 1) * points]
        rows[spans + 1, 0:1, lanes] = one[6:7, 0:points] + F32(offset * size_y)
        rows[spans + 1, 1:2, lanes] = one[6:7, points : 2 * points]
    for x in range(size_x + sides * HALO):
        if x < size_x:
            kap, sig = kappa.at[x], sigma.at[x]
        else:
            slab = slabs[(x - size_x) // HALO]
            kap, sig = slab.at[0, (x - size_x) % HALO], slab.at[1, (x - size_x) % HALO]
        to_upper[x, 0:HALO] = kap[size_y - HALO :]
        to_upper[x, HALO:] = sig[size_y - HALO :]
        to_lower[x, 0:HALO] = kap[0:HALO]
        to_lower[x, HALO:] = sig[0:HALO]


def spread(spans, rows, out, start_x, planes, ext_y, size_z):
    height = planes * ext_y
    shift = start_x * ext_y
    points = rows.shape[2] // 4 * 3
    px = rows[spans, 3:4, 0:points]
    py = rows[spans + 1, 0:1, 0:points]
    pz = rows[spans + 1, 1:2, 0:points]
    size_y = ext_y - 2 * HALO
    y_row = lax.broadcasted_iota(jnp.int32, (ext_y, points), 0)
    y_cell = jnp.where(y_row < size_y + HALO, y_row, y_row - ext_y).astype(F32)
    by = bump(y_cell - py)
    x_cell = (lax.broadcasted_iota(jnp.int32, (planes, points), 0) + start_x).astype(F32)
    bx = bump(x_cell - px)
    z_cell = lax.broadcasted_iota(jnp.int32, (size_z, points), 0) + lax.axis_index("vert") * size_z
    bz_high, bz_low = two_parts(bump(z_cell.astype(F32) - pz))
    cross = jnp.concatenate([by * bx[x : x + 1] for x in range(planes)], axis=0)
    for c in range(3):
        high, low = two_parts(cross * rows[spans, c : c + 1, 0:points])
        out[c] = dot_lanes(high, bz_high) + dot_lanes(low, bz_high) + dot_lanes(high, bz_low)

    gates = rows.shape[2]
    chunk = 512
    row_id = lax.broadcasted_iota(jnp.int32, (height, chunk), 0)
    z_id = lax.broadcasted_iota(jnp.int32, (size_z, chunk), 0)

    def one_chunk(step, carry):
        j = step // (gates // chunk)
        lanes = pl.ds(pl.multiple_of(step % (gates // chunk) * chunk, chunk), chunk)
        place = rows[j, 3:4, lanes].astype(jnp.int32)
        line = (place >> (size_z.bit_length() - 1)) - shift
        line = jnp.where(place < 0, -1, line)
        pick = jnp.where(row_id == line, 1.0, 0.0).astype(BF16)
        pick_z = jnp.where(z_id == (place & (size_z - 1)), 1.0, 0.0).astype(BF16)
        for c in range(3):
            high, low = two_parts(rows[j, c : c + 1, lanes])
            out[c] += dot_lanes(pick * high, pick_z) + dot_lanes(pick * low, pick_z)
        return carry

    lax.fori_loop(0, spans * (gates // chunk), one_chunk, 0)


def own_kernel(spans, size_x, ext_y, size_z, rows, out):
    spread(spans, rows, out, 0, size_x, ext_y, size_z)


def extend_kernel(spans, sides, *refs):
    others = refs[:sides]
    own, kappa, sigma = refs[sides : sides + 3]
    slabs = refs[sides + 3 : 2 * sides + 3]
    upper, lower = refs[2 * sides + 3 : 2 * sides + 5]
    source, kappa_ext, face = refs[2 * sides + 5 : 2 * sides + 8]
    strips = refs[2 * sides + 8 :]
    size_x, size_y, size_z = kappa.shape
    ext_y = size_y + 2 * HALO
    if sides == 1:
        starts = [jnp.where(lax.axis_index("stream") == 0, 0, size_x - HALO)]
    else:
        starts = [0, size_x - HALO]
    for rows, strip, start in zip(others, strips, starts):
        spread(spans, rows, strip, start, HALO, ext_y, size_z)
    lanes = face.shape[3]
    side = pl.ds(pl.multiple_of(jnp.where(lax.axis_index("vert") == 0, size_z - lanes, 0), lanes), lanes)
    for x in range(size_x + sides * HALO):
        if x < size_x:
            kap, sig = kappa[x], sigma[x]
        else:
            slab = slabs[(x - size_x) // HALO]
            kap, sig = slab[0, (x - size_x) % HALO], slab[1, (x - size_x) % HALO]
        kappa_ext[x] = jnp.concatenate([kap, upper[x, 0:HALO], lower[x, 0:HALO]], axis=0)
        sig = jnp.concatenate([sig, upper[x, HALO:], lower[x, HALO:]], axis=0)
        for c in range(3):
            if x < size_x:
                value = own[c, x * ext_y : (x + 1) * ext_y, :]
            else:
                place = (x - size_x) % HALO * ext_y
                value = strips[(x - size_x) // HALO][c, place : place + ext_y, :]
            source[c, x] = value * sig
            face[c, x] = source[c, x, :, side]
        face[3, x] = kappa_ext[x, :, side]


def diffuse_kernel(sides, source, kappa_ext, face, out, ping, pong, root, ax, ay, aym, az, azm, keep):
    planes, ext_y, size_z = kappa_ext.shape
    size_x, size_y = out.shape[1], out.shape[2]
    lanes = face.shape[3]
    ext_z = size_z + lanes
    stream, vert = lax.axis_index("stream"), lax.axis_index("vert")

    def fill(x, carry):
        for c in range(3):
            ping[c, x, :, 0:size_z] = source[c, x]
            ping[c, x, :, size_z:] = face[c, x]
        root[x, :, 0:size_z] = jnp.sqrt(kappa_ext[x])
        root[x, :, size_z:] = jnp.sqrt(face[3, x])
        return carry

    lax.fori_loop(0, planes, fill, 0)
    lane = lax.broadcasted_iota(jnp.int32, (ext_y, ext_z), 1)
    wall_z = jnp.where(lane == jnp.where(vert == 0, ext_z - 1, size_z - 1), 0.0, 1.0)
    last = lax.axis_size("stream") - 1

    def faces(x, carry):
        after = jnp.where(x == planes - 1, 0, x + 1)
        here = root[x]
        if sides == 1:
            wall = ((x == planes - 1) & (stream == 0)) | ((x == size_x - 1) & (stream == 1))
        else:
            wall = ((x == planes - 1) & (stream == 0)) | ((x == size_x - 1) & (stream == last))
        ax[x] = here * root[after] * jnp.where(wall, 0.0, 1.0)
        up = here * pltpu.roll(here, ext_y - 1, 0)
        ay[x] = up
        aym[x] = pltpu.roll(up, 1, 0)
        up = here * pltpu.roll(here, ext_z - 1, 1) * wall_z
        az[x] = up
        azm[x] = pltpu.roll(up, 1, 1)
        return carry

    lax.fori_loop(0, planes, faces, 0)

    def total(x, carry):
        before = jnp.where(x == 0, planes - 1, x - 1)
        keep[x] = 1.0 - (ax[x] + ax[before] + ay[x] + aym[x] + az[x] + azm[x])
        return carry

    lax.fori_loop(0, planes, total, 0)

    for p in range(PASSES):
        deep = PASSES - 1 - p
        old, new = (ping, pong) if p % 2 == 0 else (pong, ping)
        first = jnp.where(stream == 0, 0, planes - deep) if sides == 1 else planes - deep

        def one_plane(i, carry, old=old, new=new, first=first, p=p):
            x = i + first
            x = jnp.where(x >= planes, x - planes, x)
            after = jnp.where(x == planes - 1, 0, x + 1)
            before = jnp.where(x == 0, planes - 1, x - 1)
            for c in range(3):
                value = old[c, x]
                moved = keep[x] * value
                moved += ax[x] * old[c, after] + ax[before] * old[c, before]
                moved += ay[x] * pltpu.roll(value, ext_y - 1, 0) + aym[x] * pltpu.roll(value, 1, 0)
                moved += az[x] * pltpu.roll(value, ext_z - 1, 1) + azm[x] * pltpu.roll(value, 1, 1)
                if p == PASSES - 1:
                    out[c, x] = moved[0:size_y, 0:size_z]
                else:
                    new[c, x] = moved
            return carry

        lax.fori_loop(0, size_x + sides * deep, one_plane, 0)


def call(kernel, outs, scratch, flops, *args):
    moved = sum(4 * a.size for a in args) + sum(4 * o.size for o in outs)
    return pl.pallas_call(
        kernel,
        out_shape=outs,
        in_specs=[pl.BlockSpec(memory_space=pltpu.VMEM)] * len(args),
        out_specs=[pl.BlockSpec(memory_space=pltpu.VMEM)] * len(outs),
        scratch_shapes=scratch,
        compiler_params=pltpu.CompilerParams(vmem_limit_bytes=56 * 1024 * 1024),
        cost_estimate=pl.CostEstimate(flops=flops, bytes_accessed=moved, transcendentals=0),
    )(*args)


def ring(array, step):
    count = lax.axis_size("span")
    return lax.ppermute(array, "span", [(i, (i + step) % count) for i in range(count)])


def across_bands(arrays):
    count = lax.axis_size("stream")
    if count == 2:
        return [lax.ppermute(arrays[0], "stream", [(0, 1), (1, 0)])]
    return [
        lax.ppermute(arrays[1], "stream", [(i + 1, i) for i in range(count - 1)]),
        lax.ppermute(arrays[0], "stream", [(i, i + 1) for i in range(count - 1)]),
    ]


def on_device(
    kappa,
    sigma,
    gate_residual,
    gate_azimuth,
    gate_elevation,
    gate_brick,
    gate_cell,
    blade_force,
    point_x,
    point_y,
    point_z,
):
    size_x, size_y, size_z = kappa.shape
    spans = lax.axis_size("span")
    sides = 1 if lax.axis_size("stream") == 2 else 2
    gates = gate_residual.shape[2]
    lanes = 128
    ext_x, ext_y = size_x + sides * HALO, size_y + 2 * HALO
    shape = lambda *dims: jax.ShapeDtypeStruct(dims, F32)
    payload, *slabs = call(
        functools.partial(pack_kernel, sides),
        [shape(8, gates)] + [shape(2, HALO, size_y, size_z)] * sides,
        [],
        1000,
        gate_residual,
        gate_azimuth,
        gate_elevation,
        gate_brick.reshape(1, gates),
        gate_cell,
        blade_force,
        point_x,
        point_y,
        point_z,
        kappa,
        sigma,
    )
    if spans == 4:
        payloads = [payload, ring(payload, 1), ring(payload, -1), ring(payload, 2)]
    else:
        gathered = lax.all_gather(payload, "span")
        payloads = [jnp.roll(gathered, -lax.axis_index("span"), axis=0)]
    slabs = across_bands(slabs)
    rows, to_upper, to_lower = call(
        functools.partial(sort_kernel, spans, sides, len(payloads)),
        [shape(spans + 2, 4, gates), shape(ext_x, 2 * HALO, size_z), shape(ext_x, 2 * HALO, size_z)],
        [],
        1000,
        *payloads,
        kappa,
        sigma,
        *slabs,
    )
    others = across_bands([rows] * sides)
    from_lower, from_upper = ring(to_upper, 1), ring(to_lower, -1)
    (own,) = call(
        functools.partial(own_kernel, spans, size_x, ext_y, size_z),
        [shape(3, size_x * ext_y, size_z)],
        [],
        12 * size_x * ext_y * size_z * spans * gates,
        rows,
    )
    source, kappa_ext, face = call(
        functools.partial(extend_kernel, spans, sides),
        [shape(3, ext_x, ext_y, size_z), shape(ext_x, ext_y, size_z), shape(4, ext_x, ext_y, lanes)],
        [pltpu.VMEM((3, HALO * ext_y, size_z), F32)] * sides,
        12 * HALO * ext_y * size_z * spans * gates,
        *others,
        own,
        kappa,
        sigma,
        *slabs,
        from_upper,
        from_lower,
    )
    face = lax.ppermute(face, "vert", [(0, 1), (1, 0)])
    wide = (ext_x, ext_y, size_z + lanes)
    (field,) = call(
        functools.partial(diffuse_kernel, sides),
        [shape(3, size_x, size_y, size_z)],
        [pltpu.VMEM((3, *wide), F32)] * 2 + [pltpu.VMEM(wide, F32)] * 7,
        60 * 3 * ext_x * ext_y * size_z,
        source,
        kappa_ext,
        face,
    )
    return field


def solution(mesh):
    placed = (
        P(("grp", "stream"), "span", "vert"),
        P(("grp", "stream"), "span", "vert"),
        P(("grp", "stream"), "vert", "span"),
        P(("grp", "stream"), "vert", "span"),
        P(("grp", "stream"), "vert", "span"),
        P(("grp", "stream"), "vert", "span", None),
        P(("grp", "stream"), "vert", "span"),
        P(None, ("grp", "stream"), "span"),
        P(("grp", "stream"), "span"),
        P(("grp", "stream"), "span"),
        P(("grp", "stream"), "span"),
    )
    return jax.shard_map(
        on_device,
        mesh=mesh,
        in_specs=placed,
        out_specs=P(None, ("grp", "stream"), "span", "vert"),
        check_vma=False,
    )
```

```python
import functools

import jax
import jax.numpy as jnp
from jax import lax
from jax.experimental import pallas as pl
from jax.experimental.pallas import tpu as pltpu
from jax.sharding import PartitionSpec as P

SPREAD = 6
PASSES = 4
HALO = 4
BF16 = jnp.bfloat16
F32 = jnp.float32
CONTRACT_LANES = (((1,), (1,)), ((), ()))


def bump(distance):
    scaled = distance * F32(1.0 / SPREAD)
    return jnp.square(jnp.maximum(0.0, 1.0 - scaled * scaled))


def two_parts(values):
    high = values.astype(BF16)
    return high, (values - high.astype(F32)).astype(BF16)


def dot_lanes(left, right):
    return lax.dot_general(left, right, CONTRACT_LANES, preferred_element_type=F32)


def pack_kernel(residual, azimuth, elevation, brick, cell, force, px, py, pz, kappa, sigma, payload, to_upper, to_lower):
    cosine = jnp.cos(elevation[0])
    value = residual[0]
    payload[0:1, :] = cosine * jnp.cos(azimuth[0]) * value
    payload[1:2, :] = cosine * jnp.sin(azimuth[0]) * value
    payload[2:3, :] = jnp.sin(elevation[0]) * value
    payload[3:4, :] = brick[...].astype(F32)
    payload[4:5, :] = cell[0].astype(F32)
    points = px.shape[1]
    payload[5:8, :] = jnp.zeros((3, payload.shape[1]), F32)
    for c in range(3):
        payload[5:6, c * points : (c + 1) * points] = force[c]
    payload[5:6, 3 * points : 4 * points] = px[...]
    payload[6:7, 0:points] = py[...]
    payload[6:7, points : 2 * points] = pz[...]
    size_y = kappa.shape[1]
    to_upper[:, 0:HALO] = kappa[:, size_y - HALO :]
    to_upper[:, HALO:] = sigma[:, size_y - HALO :]
    to_lower[:, 0:HALO] = kappa[:, 0:HALO]
    to_lower[:, HALO:] = sigma[:, 0:HALO]


def lines_of(payload, spans, start_x, size_y, size_z):
    brick = payload[3:4, :].astype(jnp.int32)
    cell = payload[4:5, :].astype(jnp.int32)
    away = brick - lax.axis_index("span")
    away = jnp.where(away < 0, away + spans, away)
    x = cell // (size_y * size_z)
    y = cell // size_z % size_y
    upper = (away == 1) & (y < HALO)
    lower = (away == spans - 1) & (y >= size_y - HALO)
    row = jnp.where(away == 0, y, jnp.where(upper, y + size_y, jnp.where(lower, y + 2 * HALO, -1)))
    return jnp.where(row < 0, -1, (x - start_x) * (size_y + 2 * HALO) + row), cell % size_z


def spread(payload_of, spans, sources, near, out, start_x, planes, size_y, size_z, first, unroll=False):
    ext_y = size_y + 2 * HALO
    height = planes * ext_y
    points = payload_of(0).shape[1] // 4
    count = len(near) * points
    rows = [[payload_of(j)[r : r + 1, :] for r in (5, 6)] for j, _ in near]

    def joined(r, k):
        return jnp.concatenate([pair[r][:, k * points : (k + 1) * points] for pair in rows], axis=1)

    px, pz = joined(0, 3), joined(1, 1)
    py = jnp.concatenate(
        [pair[1][:, 0:points] + F32(side * size_y) for pair, (_, side) in zip(rows, near)], axis=1
    )
    y_row = lax.broadcasted_iota(jnp.int32, (ext_y, count), 0)
    by = bump(jnp.where(y_row < size_y + HALO, y_row, y_row - ext_y).astype(F32) - py)
    x_cell = (lax.broadcasted_iota(jnp.int32, (planes, count), 0) + start_x).astype(F32)
    bx = bump(x_cell - px)
    z_cell = lax.broadcasted_iota(jnp.int32, (size_z, count), 0) + lax.axis_index("vert") * size_z
    bz_high, bz_low = two_parts(bump(z_cell.astype(F32) - pz))
    cross = jnp.concatenate([by * bx[x : x + 1] for x in range(planes)], axis=0)
    parts = [two_parts(cross * joined(0, c)) for c in range(3)]
    by_high = dot_lanes(jnp.concatenate([part for pair in parts for part in pair], axis=0), bz_high)
    by_low = dot_lanes(jnp.concatenate([high for high, _ in parts], axis=0), bz_low)
    for c in range(3):
        high = 2 * c * height
        both = by_high[high : high + height] + by_high[high + height : high + 2 * height]
        both += by_low[c * height : (c + 1) * height]
        out[c] = both if first is None else first[c] + both

    gates = payload_of(0).shape[1]
    row_id = lax.broadcasted_iota(jnp.int32, (height, gates), 0)
    z_id = lax.broadcasted_iota(jnp.int32, (size_z, gates), 0)

    def one_source(j, carry):
        one = payload_of(j)
        line, z = lines_of(one, spans, start_x, size_y, size_z)
        pick = jnp.where(row_id == line, 1.0, 0.0).astype(BF16)
        pick_z = jnp.where(z_id == z, 1.0, 0.0).astype(BF16)
        parts = [part for c in range(3) for part in two_parts(one[c : c + 1, :])]
        sums = dot_lanes(jnp.concatenate([pick * part for part in parts], axis=0), pick_z)
        for c in range(3):
            high = 2 * c * height
            out[c] += sums[high : high + height] + sums[high + height : high + 2 * height]
        return carry

    if unroll:
        for j in range(*sources):
            one_source(j, 0)
    else:
        lax.fori_loop(*sources, one_source, 0)


def near_of(spans):
    return ((0, 0), (1, -1), (2, 1)) if spans == 4 else ((0, 0), (spans - 1, -1), (1, 1))


def first_kernel(spans, dims, payload, out):
    size_x, size_y, size_z = dims
    spread(lambda j: payload, spans, (0, 1), near_of(spans)[:1], out, 0, size_x, size_y, size_z, None, unroll=True)


def second_kernel(spans, dims, count, *refs):
    payloads, (first, out) = refs[:count], refs[count:]
    size_x, size_y, size_z = dims
    near = near_of(spans)[1:]
    pick = (lambda j: payloads[j]) if count > 1 else (lambda j: payloads[0].at[j])
    spread(pick, spans, (1, spans), near, out, 0, size_x, size_y, size_z, first, unroll=count > 1)


def bands_kernel(sides, count, *refs):
    payloads = refs[:count]
    kappa, sigma, upper, lower = refs[count : count + 4]
    outs = refs[count + 4 : count + 4 + sides]
    size_x, size_y, size_z = kappa.shape
    ext_y = size_y + 2 * HALO
    if sides == 1:
        starts = [jnp.where(lax.axis_index("stream") == 0, size_x - HALO, 0)]
    else:
        starts = [size_x - HALO, 0]
    for out, start in zip(outs, starts):
        places = [(payload, None) for payload in payloads] if count > 1 else [(payloads[0], j) for j in range(payloads[0].shape[0])]
        for j, (payload, k) in enumerate(places):
            one = payload[...] if k is None else payload[k]
            for part in range(one.shape[1] // size_z):
                out[j * one.shape[1] // size_z + part] = one[:, part * size_z : (part + 1) * size_z]
        base = out.shape[0] - HALO * 2 * ext_y // 8
        for i in range(HALO):
            rows = [kappa[start + i], upper[start + i, 0:HALO], lower[start + i, 0:HALO]]
            rows += [sigma[start + i], upper[start + i, HALO:], lower[start + i, HALO:]]
            rows = jnp.concatenate(rows, axis=0)
            for part in range(2 * ext_y // 8):
                out[base + i * (2 * ext_y // 8) + part] = rows[8 * part : 8 * part + 8]


def extend_kernel(spans, sides, *refs):
    others = refs[:sides]
    behind = refs[sides : sides + 5]
    source, kappa_ext, face = refs[sides + 5 : sides + 8]
    strips = refs[sides + 8 : 2 * sides + 8]
    held = refs[2 * sides + 8 : -1]
    copies = [pltpu.make_async_copy(a, b, refs[-1].at[i]) for i, (a, b) in enumerate(zip(behind, held))]
    for copy in copies:
        copy.start()
    own, kappa, sigma, upper, lower = held
    size_x, size_y, size_z = kappa.shape
    ext_y = size_y + 2 * HALO
    parts = others[0].shape[0] - HALO * 2 * ext_y // 8
    if sides == 1:
        starts = [jnp.where(lax.axis_index("stream") == 0, 0, size_x - HALO)]
    else:
        starts = [0, size_x - HALO]
    for packed, strip, start in zip(others, strips, starts):

        def payload_of(j, packed=packed):
            each = parts // spans
            return jnp.concatenate([packed[j * each + part] for part in range(each)], axis=1)

        spread(payload_of, spans, (0, spans), near_of(spans), strip, start, HALO, size_y, size_z, None)
    for copy in copies:
        copy.wait()
    vert = lax.axis_index("vert")
    side = pl.ds(pl.multiple_of(jnp.where(vert == 0, size_z - 128, 0), 128), 128)
    for x in range(size_x + sides * HALO):
        if x < size_x:
            kappa_ext[x] = jnp.concatenate([kappa[x], upper[x, 0:HALO], lower[x, 0:HALO]], axis=0)
            sig = jnp.concatenate([sigma[x], upper[x, HALO:], lower[x, HALO:]], axis=0)
        else:
            packed = others[(x - size_x) // HALO]
            tiles = ext_y // 8
            base = parts + (x - size_x) % HALO * 2 * tiles
            kappa_ext[x] = jnp.concatenate([packed[base + k] for k in range(tiles)], axis=0)
            sig = jnp.concatenate([packed[base + tiles + k] for k in range(tiles)], axis=0)
        for c in range(3):
            if x < size_x:
                value = own[c, x * ext_y : (x + 1) * ext_y, :]
            else:
                place = (x - size_x) % HALO * ext_y
                value = strips[(x - size_x) // HALO][c, place : place + ext_y, :]
            source[c, x] = value * sig
    lane = lax.broadcasted_iota(jnp.int32, (8, 128), 1)
    tiles = face_tiles(size_x + sides * HALO, ext_y)
    for g in range(0, len(tiles), 16):
        packed = jnp.zeros((8, 128), F32)
        for k, (c, x, y) in enumerate(tiles[g : g + 16]):
            tile = kappa_ext[x, y : y + 8, side] if c == 3 else source[c, x, y : y + 8, side]
            turned = pltpu.roll(tile, (8 * k + 8 * (1 - vert)) & 127, 1)
            packed = jnp.where(lane // 8 == k, turned, packed)
        face[g // 16] = packed


def face_tiles(planes, ext_y):
    return [(c, x, y) for c in range(4) for x in range(planes) for y in range(0, ext_y, 8)]


def lanes_on(values, step, lane):
    tiles = [values[:, k : k + 128] for k in range(0, values.shape[1], 128)]
    turned = [pltpu.roll(tile, step % 128, 1) for tile in tiles]
    edge = lane == (0 if step == 1 else 127)
    return jnp.concatenate(
        [jnp.where(edge, turned[(k - step) % len(tiles)], turned[k]) for k in range(len(tiles))], axis=1
    )


def each_plane(count, step, unroll=4):
    whole = count // unroll * unroll
    lax.fori_loop(0, whole, lambda i, carry: (step(i), carry)[1], 0, unroll=unroll)
    for i in range(whole, count):
        step(i)


def diffuse_kernel(sides, source, kappa_ext, face, out, ping, pong, root, ax, ay, aym, az, azm, keep):
    planes, ext_y, size_z = kappa_ext.shape
    size_x, size_y = out.shape[1], out.shape[2]
    ext_z = size_z + 128
    stream, vert = lax.axis_index("stream"), lax.axis_index("vert")

    def fill(x):
        for c in range(3):
            ping[c, x, :, 0:size_z] = source[c, x]
        root[x, :, 0:size_z] = jnp.sqrt(kappa_ext[x])

    each_plane(planes, fill)
    lane = lax.broadcasted_iota(jnp.int32, (ext_y, 128), 1)
    known = lax.broadcasted_iota(jnp.int32, (8, 128), 1) // 8 == vert * 15
    for t, (c, x, y) in enumerate(face_tiles(planes, ext_y)):
        turned = pltpu.roll(face[t // 16], (256 - 8 * (t % 16) - 8 * vert) & 127, 1)
        if c == 3:
            root[x, y : y + 8, size_z:] = jnp.sqrt(jnp.where(known, turned, 0.0))
        else:
            ping[c, x, y : y + 8, size_z:] = turned
    last = lax.axis_size("stream") - 1

    def faces(x):
        after = jnp.where(x == planes - 1, 0, x + 1)
        here = root[x]
        wall = ((x == planes - 1) & (stream == 0)) | ((x == size_x - 1) & (stream == last))
        ax[x] = here * root[after] * jnp.where(wall, 0.0, 1.0)
        up = here * pltpu.roll(here, ext_y - 1, 0)
        ay[x] = up
        aym[x] = pltpu.roll(up, 1, 0)
        up = here * lanes_on(here, -1, lane)
        az[x] = up
        azm[x] = lanes_on(up, 1, lane)

    each_plane(planes, faces)

    def total(x):
        before = jnp.where(x == 0, planes - 1, x - 1)
        keep[x] = 1.0 - (ax[x] + ax[before] + ay[x] + aym[x] + az[x] + azm[x])

    each_plane(planes, total)

    for p in range(PASSES):
        deep = PASSES - 1 - p
        old, new = (ping, pong) if p % 2 == 0 else (pong, ping)
        first = jnp.where(stream == 0, 0, planes - deep) if sides == 1 else planes - deep

        def one_plane(i, old=old, new=new, first=first, p=p):
            x = i + first
            x = jnp.where(x >= planes, x - planes, x)
            after = jnp.where(x == planes - 1, 0, x + 1)
            before = jnp.where(x == 0, planes - 1, x - 1)
            for c in range(3):
                value = old[c, x]
                moved = keep[x] * value
                moved += ax[x] * old[c, after] + ax[before] * old[c, before]
                moved += ay[x] * pltpu.roll(value, ext_y - 1, 0) + aym[x] * pltpu.roll(value, 1, 0)
                moved += az[x] * lanes_on(value, -1, lane) + azm[x] * lanes_on(value, 1, lane)
                if p == PASSES - 1:
                    out[c, x] = moved[0:size_y, 0:size_z]
                else:
                    new[c, x] = moved

        each_plane(size_x + sides * deep, one_plane)


def call(kernel, outs, scratch, flops, *args, left=(), aliases=()):
    moved = sum(4 * a.size for a in args) + sum(4 * o.size for o in outs)
    spaces = [pl.ANY if i in left else pltpu.VMEM for i in range(len(args))]
    return pl.pallas_call(
        kernel,
        out_shape=outs,
        in_specs=[pl.BlockSpec(memory_space=space) for space in spaces],
        out_specs=[pl.BlockSpec(memory_space=pltpu.VMEM)] * len(outs),
        scratch_shapes=scratch,
        input_output_aliases=dict(aliases),
        compiler_params=pltpu.CompilerParams(vmem_limit_bytes=56 * 1024 * 1024),
        cost_estimate=pl.CostEstimate(flops=flops, bytes_accessed=moved, transcendentals=0),
    )(*args)


def ring(array, step):
    count = lax.axis_size("span")
    return lax.ppermute(array, "span", [(i, (i + step) % count) for i in range(count)])


def across_bands(arrays):
    count = lax.axis_size("stream")
    if count == 2:
        return [lax.ppermute(arrays[0], "stream", [(0, 1), (1, 0)])]
    return [
        lax.ppermute(arrays[1], "stream", [(i + 1, i) for i in range(count - 1)]),
        lax.ppermute(arrays[0], "stream", [(i, i + 1) for i in range(count - 1)]),
    ]


def on_device(
    kappa,
    sigma,
    gate_residual,
    gate_azimuth,
    gate_elevation,
    gate_brick,
    gate_cell,
    blade_force,
    point_x,
    point_y,
    point_z,
):
    size_x, size_y, size_z = kappa.shape
    spans = lax.axis_size("span")
    sides = 1 if lax.axis_size("stream") == 2 else 2
    gates = gate_residual.shape[2]
    ext_x, ext_y = size_x + sides * HALO, size_y + 2 * HALO
    shape = lambda *dims: jax.ShapeDtypeStruct(dims, F32)
    payload, to_upper, to_lower = call(
        pack_kernel,
        [shape(8, gates)] + [shape(size_x, 2 * HALO, size_z)] * 2,
        [],
        1000,
        gate_residual,
        gate_azimuth,
        gate_elevation,
        gate_brick.reshape(1, gates),
        gate_cell,
        blade_force,
        point_x,
        point_y,
        point_z,
        kappa,
        sigma,
    )
    if spans == 4:
        payloads = [payload, ring(payload, 1), ring(payload, -1), ring(payload, 2)]
    else:
        payloads = [jnp.roll(lax.all_gather(payload, "span"), -lax.axis_index("span"), axis=0)]
    from_lower, from_upper = ring(to_upper, 1), ring(to_lower, -1)
    dims = (size_x, size_y, size_z)
    work = 12 * size_x * ext_y * size_z * gates
    planes = shape(3, size_x * ext_y, size_z)
    (own,) = call(functools.partial(first_kernel, spans, dims), [planes], [], work, payload)
    parts = spans * gates // size_z + HALO * 2 * ext_y // 8
    others = across_bands(
        call(
            functools.partial(bands_kernel, sides, len(payloads)),
            [shape(parts, 8, size_z)] * sides,
            [],
            1000,
            *payloads,
            kappa,
            sigma,
            from_upper,
            from_lower,
        )
    )
    (own,) = call(
        functools.partial(second_kernel, spans, dims, len(payloads)),
        [planes],
        [],
        work * (spans - 1),
        *payloads,
        own,
        aliases=((len(payloads), 0),),
    )
    behind = [own, kappa, sigma, from_upper, from_lower]
    tiles = len(face_tiles(ext_x, ext_y))
    source, kappa_ext, face = call(
        functools.partial(extend_kernel, spans, sides),
        [shape(3, ext_x, ext_y, size_z), shape(ext_x, ext_y, size_z), shape(-(-tiles // 16), 8, 128)],
        [pltpu.VMEM((3, HALO * ext_y, size_z), F32)] * sides
        + [pltpu.VMEM(a.shape, F32) for a in behind]
        + [pltpu.SemaphoreType.DMA((len(behind),))],
        work // 4 * spans,
        *others,
        *behind,
        left=range(sides, sides + len(behind)),
    )
    face = lax.ppermute(face, "vert", [(0, 1), (1, 0)])
    wide = (ext_x, ext_y, size_z + 128)
    (field,) = call(
        functools.partial(diffuse_kernel, sides),
        [shape(3, size_x, size_y, size_z)],
        [pltpu.VMEM((3, *wide), F32)] * 2 + [pltpu.VMEM(wide, F32)] * 7,
        60 * 3 * ext_x * ext_y * size_z,
        source,
        kappa_ext,
        face,
    )
    return field


def solution(mesh):
    placed = (
        P(("grp", "stream"), "span", "vert"),
        P(("grp", "stream"), "span", "vert"),
        P(("grp", "stream"), "vert", "span"),
        P(("grp", "stream"), "vert", "span"),
        P(("grp", "stream"), "vert", "span"),
        P(("grp", "stream"), "vert", "span", None),
        P(("grp", "stream"), "vert", "span"),
        P(None, ("grp", "stream"), "span"),
        P(("grp", "stream"), "span"),
        P(("grp", "stream"), "span"),
        P(("grp", "stream"), "span"),
    )
    return jax.shard_map(
        on_device,
        mesh=mesh,
        in_specs=placed,
        out_specs=P(None, ("grp", "stream"), "span", "vert"),
        check_vma=False,
    )
```

```python
import functools

import jax
import jax.numpy as jnp
from jax import lax
from jax.experimental import pallas as pl
from jax.experimental.pallas import tpu as pltpu
from jax.sharding import PartitionSpec as P

SPREAD = 6
PASSES = 4
HALO = 4
BF16 = jnp.bfloat16
F32 = jnp.float32
CONTRACT_LANES = (((1,), (1,)), ((), ()))


def bump(distance):
    scaled = distance * F32(1.0 / SPREAD)
    return jnp.square(jnp.maximum(0.0, 1.0 - scaled * scaled))


def two_parts(values):
    high = values.astype(BF16)
    return high, (values - high.astype(F32)).astype(BF16)


def dot_lanes(left, right):
    return lax.dot_general(left, right, CONTRACT_LANES, preferred_element_type=F32)


def pack_kernel(sides, *refs):
    residual, azimuth, elevation, brick, cell, force, px, py, pz, kappa, sigma = refs[:11]
    payload, to_upper, to_lower = refs[11:14]
    slabs = refs[14:]
    cosine = jnp.cos(elevation[0])
    value = residual[0]
    gates, points = value.shape[1], px.shape[1]
    rest = jnp.zeros((1, gates - 2 * points), F32)
    rows = [
        cosine * jnp.cos(azimuth[0]) * value,
        cosine * jnp.sin(azimuth[0]) * value,
        jnp.sin(elevation[0]) * value,
        brick[...].astype(F32),
        cell[0].astype(F32),
        jnp.concatenate([force[0], force[1], force[2], px[...]], axis=1),
        jnp.concatenate([py[...], pz[...], rest], axis=1),
        jnp.zeros((1, gates), F32),
    ]
    for r, row in enumerate(rows):
        payload[r : r + 1, :] = row
    size_x, size_y, size_z = kappa.shape
    to_upper[:, 0:HALO] = kappa[:, size_y - HALO :]
    to_upper[:, HALO:] = sigma[:, size_y - HALO :]
    to_lower[:, 0:HALO] = kappa[:, 0:HALO]
    to_lower[:, HALO:] = sigma[:, 0:HALO]
    for slab, start in zip(slabs, edges(sides, size_x)):
        slab[:, 0:size_y] = kappa[pl.ds(start, HALO)]
        slab[:, size_y:] = sigma[pl.ds(start, HALO)]


def edges(sides, size_x):
    if sides == 1:
        return [jnp.where(lax.axis_index("stream") == 0, size_x - HALO, 0)]
    return [size_x - HALO, 0]


def lines_of(payload, spans, start_x, size_y, size_z):
    brick = payload[3:4, :].astype(jnp.int32)
    cell = payload[4:5, :].astype(jnp.int32)
    away = brick - lax.axis_index("span")
    away = jnp.where(away < 0, away + spans, away)
    x = cell // (size_y * size_z)
    y = cell // size_z % size_y
    upper = (away == 1) & (y < HALO)
    lower = (away == spans - 1) & (y >= size_y - HALO)
    row = jnp.where(away == 0, y, jnp.where(upper, y + size_y, jnp.where(lower, y + 2 * HALO, -1)))
    return jnp.where(row < 0, -1, (x - start_x) * (size_y + 2 * HALO) + row), cell % size_z


def spread(payload_of, spans, sources, near, out, start_x, planes, size_y, size_z, first, unroll=False):
    ext_y = size_y + 2 * HALO
    height = planes * ext_y
    points = payload_of(0).shape[1] // 4
    count = len(near) * points
    rows = [[payload_of(j)[r : r + 1, :] for r in (5, 6)] for j, _ in near]

    def joined(r, k):
        return jnp.concatenate([pair[r][:, k * points : (k + 1) * points] for pair in rows], axis=1)

    px, pz = joined(0, 3), joined(1, 1)
    py = jnp.concatenate(
        [pair[1][:, 0:points] + F32(side * size_y) for pair, (_, side) in zip(rows, near)], axis=1
    )
    y_row = lax.broadcasted_iota(jnp.int32, (ext_y, count), 0)
    by = bump(jnp.where(y_row < size_y + HALO, y_row, y_row - ext_y).astype(F32) - py)
    x_cell = (lax.broadcasted_iota(jnp.int32, (planes, count), 0) + start_x).astype(F32)
    bx = bump(x_cell - px)
    z_cell = lax.broadcasted_iota(jnp.int32, (size_z, count), 0) + lax.axis_index("vert") * size_z
    bz_high, bz_low = two_parts(bump(z_cell.astype(F32) - pz))
    cross = jnp.concatenate([by * bx[x : x + 1] for x in range(planes)], axis=0)
    parts = [two_parts(cross * joined(0, c)) for c in range(3)]
    by_high = dot_lanes(jnp.concatenate([part for pair in parts for part in pair], axis=0), bz_high)
    by_low = dot_lanes(jnp.concatenate([high for high, _ in parts], axis=0), bz_low)
    for c in range(3):
        high = 2 * c * height
        both = by_high[high : high + height] + by_high[high + height : high + 2 * height]
        both += by_low[c * height : (c + 1) * height]
        out[c] = both if first is None else first[c] + both

    gates = payload_of(0).shape[1]
    row_id = lax.broadcasted_iota(jnp.int32, (height, gates), 0)
    z_id = lax.broadcasted_iota(jnp.int32, (size_z, gates), 0)

    def one_source(j, carry):
        one = payload_of(j)
        line, z = lines_of(one, spans, start_x, size_y, size_z)
        pick = jnp.where(row_id == line, 1.0, 0.0).astype(BF16)
        pick_z = jnp.where(z_id == z, 1.0, 0.0).astype(BF16)
        parts = [part for c in range(3) for part in two_parts(one[c : c + 1, :])]
        sums = dot_lanes(jnp.concatenate([pick * part for part in parts], axis=0), pick_z)
        for c in range(3):
            high = 2 * c * height
            out[c] += sums[high : high + height] + sums[high + height : high + 2 * height]
        return carry

    if unroll:
        for j in range(*sources):
            one_source(j, 0)
    else:
        lax.fori_loop(*sources, one_source, 0)


def near_of(spans):
    return ((0, 0), (1, -1), (2, 1)) if spans == 4 else ((0, 0), (spans - 1, -1), (1, 1))


def first_kernel(spans, dims, payload, out):
    size_x, size_y, size_z = dims
    spread(lambda j: payload, spans, (0, 1), near_of(spans)[:1], out, 0, size_x, size_y, size_z, None, unroll=True)


def payload_in(refs, j):
    return refs[0].at[j] if len(refs) == 1 else refs[j]


def second_kernel(spans, dims, count, *refs):
    payloads, (first, out) = refs[:count], refs[count:]
    size_x, size_y, size_z = dims
    near = near_of(spans)[1:]
    spread(lambda j: payload_in(payloads, j), spans, (1, spans), near, out, 0, size_x, size_y, size_z, first, unroll=count > 1)


def gather_kernel(count, *refs):
    for j in range(count):
        refs[count][j] = refs[j][...]


def corner_kernel(sides, upper, lower, *outs):
    for out, start in zip(outs, edges(sides, upper.shape[0])):
        out[:, 0 : 2 * HALO] = upper[pl.ds(start, HALO)]
        out[:, 2 * HALO :] = lower[pl.ds(start, HALO)]


def strip_kernel(spans, sides, dims, *refs):
    size_x, size_y, size_z = dims
    starts = edges(sides, size_x)
    starts = [size_x - HALO - starts[0]] if sides == 1 else starts[::-1]
    for payloads, strip, start in zip(refs[:sides], refs[sides:], starts):
        spread(lambda j: payloads.at[j], spans, (0, spans), near_of(spans), strip, start, HALO, size_y, size_z, None)


def extend_kernel(sides, *refs):
    own, kappa, sigma, upper, lower = refs[:5]
    strips, slabs, corners = (refs[5 + k * sides : 5 + (k + 1) * sides] for k in range(3))
    source, kappa_ext, face = refs[5 + 3 * sides :]
    size_x, size_y, size_z = kappa.shape
    ext_y = size_y + 2 * HALO
    vert = lax.axis_index("vert")
    side = pl.ds(pl.multiple_of(jnp.where(vert == 0, size_z - 128, 0), 128), 128)
    for x in range(size_x + sides * HALO):
        if x < size_x:
            kappa_ext[x] = jnp.concatenate([kappa[x], upper[x, 0:HALO], lower[x, 0:HALO]], axis=0)
            sig = jnp.concatenate([sigma[x], upper[x, HALO:], lower[x, HALO:]], axis=0)
        else:
            slab, corner = slabs[(x - size_x) // HALO], corners[(x - size_x) // HALO]
            i = (x - size_x) % HALO
            up, low = corner[i, 0 : 2 * HALO], corner[i, 2 * HALO :]
            kappa_ext[x] = jnp.concatenate([slab[i, 0:size_y], up[0:HALO], low[0:HALO]], axis=0)
            sig = jnp.concatenate([slab[i, size_y:], up[HALO:], low[HALO:]], axis=0)
        for c in range(3):
            if x < size_x:
                value = own[c, x * ext_y : (x + 1) * ext_y, :]
            else:
                place = (x - size_x) % HALO * ext_y
                value = strips[(x - size_x) // HALO][c, place : place + ext_y, :]
            source[c, x] = value * sig
    lane = lax.broadcasted_iota(jnp.int32, (8, 128), 1)
    tiles = face_tiles(size_x + sides * HALO, ext_y)
    for g in range(0, len(tiles), 16):
        packed = jnp.zeros((8, 128), F32)
        for k, (c, x, y) in enumerate(tiles[g : g + 16]):
            tile = kappa_ext[x, y : y + 8, side] if c == 3 else source[c, x, y : y + 8, side]
            turned = pltpu.roll(tile, (8 * k + 8 * (1 - vert)) & 127, 1)
            packed = jnp.where(lane // 8 == k, turned, packed)
        face[g // 16] = packed


def face_tiles(planes, ext_y):
    return [(c, x, y) for c in range(4) for x in range(planes) for y in range(0, ext_y, 8)]


def lanes_on(values, step, lane):
    tiles = [values[:, k : k + 128] for k in range(0, values.shape[1], 128)]
    turned = [pltpu.roll(tile, step % 128, 1) for tile in tiles]
    edge = lane == (0 if step == 1 else 127)
    return jnp.concatenate(
        [jnp.where(edge, turned[(k - step) % len(tiles)], turned[k]) for k in range(len(tiles))], axis=1
    )


def each_plane(count, step, unroll=4):
    whole = count // unroll * unroll
    lax.fori_loop(0, whole, lambda i, carry: (step(i), carry)[1], 0, unroll=unroll)
    for i in range(whole, count):
        step(i)


def diffuse_kernel(sides, source, kappa_ext, face, out, ping, pong, root, ax, ay, aym, az, azm, keep):
    planes, ext_y, size_z = kappa_ext.shape
    size_x, size_y = out.shape[1], out.shape[2]
    ext_z = size_z + 128
    stream, vert = lax.axis_index("stream"), lax.axis_index("vert")

    def fill(x):
        for c in range(3):
            ping[c, x, :, 0:size_z] = source[c, x]
        root[x, :, 0:size_z] = jnp.sqrt(kappa_ext[x])

    each_plane(planes, fill)
    for x in range(size_x, planes):
        for c in range(3):
            pong[c, x] = jnp.zeros((ext_y, ext_z), F32)
    lane = lax.broadcasted_iota(jnp.int32, (ext_y, 128), 1)
    known = lax.broadcasted_iota(jnp.int32, (8, 128), 1) // 8 == vert * 15
    for t, (c, x, y) in enumerate(face_tiles(planes, ext_y)):
        turned = pltpu.roll(face[t // 16], (256 - 8 * (t % 16) - 8 * vert) & 127, 1)
        if c == 3:
            root[x, y : y + 8, size_z:] = jnp.sqrt(jnp.where(known, turned, 0.0))
        else:
            ping[c, x, y : y + 8, size_z:] = turned
    last = lax.axis_size("stream") - 1

    def faces(x):
        after = jnp.where(x == planes - 1, 0, x + 1)
        here = root[x]
        wall = ((x == planes - 1) & (stream == 0)) | ((x == size_x - 1) & (stream == last))
        ax[x] = here * root[after] * jnp.where(wall, 0.0, 1.0)
        up = here * pltpu.roll(here, ext_y - 1, 0)
        ay[x] = up
        aym[x] = pltpu.roll(up, 1, 0)
        up = here * lanes_on(here, -1, lane)
        az[x] = up
        azm[x] = lanes_on(up, 1, lane)

    each_plane(planes, faces)

    def total(x):
        before = jnp.where(x == 0, planes - 1, x - 1)
        keep[x] = 1.0 - (ax[x] + ax[before] + ay[x] + aym[x] + az[x] + azm[x])

    each_plane(planes, total)

    for p in range(PASSES):
        deep = PASSES - 1 - p
        old, new = (ping, pong) if p % 2 == 0 else (pong, ping)
        first = jnp.where(stream == 0, 0, planes - deep) if sides == 1 else planes - deep

        def one_plane(i, old=old, new=new, first=first, p=p):
            x = i + first
            x = jnp.where(x >= planes, x - planes, x)
            after = jnp.where(x == planes - 1, 0, x + 1)
            before = jnp.where(x == 0, planes - 1, x - 1)
            for c in range(3):
                value = old[c, x]
                moved = keep[x] * value
                moved += ax[x] * old[c, after] + ax[before] * old[c, before]
                moved += ay[x] * pltpu.roll(value, ext_y - 1, 0) + aym[x] * pltpu.roll(value, 1, 0)
                moved += az[x] * lanes_on(value, -1, lane) + azm[x] * lanes_on(value, 1, lane)
                if p == PASSES - 1:
                    out[c, x] = moved[0:size_y, 0:size_z]
                else:
                    new[c, x] = moved

        each_plane(size_x + sides * deep, one_plane)


def call(kernel, outs, scratch, flops, *args, left=(), aliases=(), room=8):
    moved = sum(4 * a.size for a in args) + sum(4 * o.size for o in outs)
    spaces = [pltpu.HBM if i in left else pltpu.VMEM for i in range(len(args))]
    return pl.pallas_call(
        kernel,
        out_shape=outs,
        in_specs=[pl.BlockSpec(memory_space=space) for space in spaces],
        out_specs=[pl.BlockSpec(memory_space=pltpu.VMEM)] * len(outs),
        scratch_shapes=scratch,
        input_output_aliases=dict(aliases),
        compiler_params=pltpu.CompilerParams(vmem_limit_bytes=room * 1024 * 1024),
        cost_estimate=pl.CostEstimate(flops=flops, bytes_accessed=moved, transcendentals=0),
    )(*args)


def ring(array, step):
    count = lax.axis_size("span")
    return lax.ppermute(array, "span", [(i, (i + step) % count) for i in range(count)])


def across_bands(arrays):
    count = lax.axis_size("stream")
    if count == 2:
        return [lax.ppermute(arrays[0], "stream", [(0, 1), (1, 0)])]
    return [
        lax.ppermute(arrays[1], "stream", [(i + 1, i) for i in range(count - 1)]),
        lax.ppermute(arrays[0], "stream", [(i, i + 1) for i in range(count - 1)]),
    ]


def on_device(
    kappa,
    sigma,
    gate_residual,
    gate_azimuth,
    gate_elevation,
    gate_brick,
    gate_cell,
    blade_force,
    point_x,
    point_y,
    point_z,
):
    size_x, size_y, size_z = kappa.shape
    spans = lax.axis_size("span")
    sides = 1 if lax.axis_size("stream") == 2 else 2
    gates = gate_residual.shape[2]
    ext_x, ext_y = size_x + sides * HALO, size_y + 2 * HALO
    shape = lambda *dims: jax.ShapeDtypeStruct(dims, F32)
    inputs = [
        gate_residual,
        gate_azimuth,
        gate_elevation,
        gate_brick.reshape(1, gates),
        gate_cell,
        blade_force,
        point_x,
        point_y,
        point_z,
        kappa,
        sigma,
    ]
    payload, to_upper, to_lower, *slabs = call(
        functools.partial(pack_kernel, sides),
        [shape(8, gates)] + [shape(size_x, 2 * HALO, size_z)] * 2 + [shape(HALO, 2 * size_y, size_z)] * sides,
        [],
        1000,
        *inputs,
        room=56,
    )
    if spans == 4:
        payloads = [payload, ring(payload, 1), ring(payload, -1), ring(payload, 2)]
    else:
        payloads = [jnp.roll(lax.all_gather(payload, "span"), -lax.axis_index("span"), axis=0)]
    slabs = across_bands(slabs)
    from_lower, from_upper = ring(to_upper, 1), ring(to_lower, -1)
    dims = (size_x, size_y, size_z)
    work = 12 * size_x * ext_y * size_z * gates
    planes = shape(3, size_x * ext_y, size_z)
    (own,) = call(functools.partial(first_kernel, spans, dims), [planes], [], work, payload, room=24)
    gathered = payloads if len(payloads) == 1 else call(
        functools.partial(gather_kernel, spans), [shape(spans, 8, gates)], [], 1000, *payloads
    )
    others = across_bands(gathered * sides)
    (own,) = call(
        functools.partial(second_kernel, spans, dims, len(payloads)),
        [planes],
        [],
        work * (spans - 1),
        *payloads,
        own,
        aliases=((len(payloads), 0),),
        room=24,
    )
    corners = across_bands(
        call(
            functools.partial(corner_kernel, sides),
            [shape(HALO, 4 * HALO, size_z)] * sides,
            [],
            1000,
            from_upper,
            from_lower,
        )
    )
    strips = call(
        functools.partial(strip_kernel, spans, sides, dims),
        [shape(3, HALO * ext_y, size_z)] * sides,
        [],
        work // 4 * spans,
        *others,
        room=24,
    )
    tiles = len(face_tiles(ext_x, ext_y))
    source, kappa_ext, face = call(
        functools.partial(extend_kernel, sides),
        [shape(3, ext_x, ext_y, size_z), shape(ext_x, ext_y, size_z), shape(-(-tiles // 16), 8, 128)],
        [],
        1000,
        own,
        kappa,
        sigma,
        from_upper,
        from_lower,
        *strips,
        *slabs,
        *corners,
    )
    face = lax.ppermute(face, "vert", [(0, 1), (1, 0)])
    wide = (ext_x, ext_y, size_z + 128)
    (field,) = call(
        functools.partial(diffuse_kernel, sides),
        [shape(3, size_x, size_y, size_z)],
        [pltpu.VMEM((3, *wide), F32)] * 2 + [pltpu.VMEM(wide, F32)] * 7,
        60 * 3 * ext_x * ext_y * size_z,
        source,
        kappa_ext,
        face,
        room=20,
    )
    return field


def solution(mesh):
    placed = (
        P(("grp", "stream"), "span", "vert"),
        P(("grp", "stream"), "span", "vert"),
        P(("grp", "stream"), "vert", "span"),
        P(("grp", "stream"), "vert", "span"),
        P(("grp", "stream"), "vert", "span"),
        P(("grp", "stream"), "vert", "span", None),
        P(("grp", "stream"), "vert", "span"),
        P(None, ("grp", "stream"), "span"),
        P(("grp", "stream"), "span"),
        P(("grp", "stream"), "span"),
        P(("grp", "stream"), "span"),
    )
    return jax.shard_map(
        on_device,
        mesh=mesh,
        in_specs=placed,
        out_specs=P(None, ("grp", "stream"), "span", "vert"),
        check_vma=False,
    )
```

```python
import functools

import jax
import jax.numpy as jnp
from jax import lax
from jax.experimental import pallas as pl
from jax.experimental.pallas import tpu as pltpu
from jax.sharding import PartitionSpec as P

SPREAD = 6
PASSES = 4
HALO = 4
BF16 = jnp.bfloat16
F32 = jnp.float32
CONTRACT_LANES = (((1,), (1,)), ((), ()))


def bump(distance):
    scaled = distance * F32(1.0 / SPREAD)
    return jnp.square(jnp.maximum(0.0, 1.0 - scaled * scaled))


def two_parts(values):
    high = values.astype(BF16)
    return high, (values - high.astype(F32)).astype(BF16)


def dot_lanes(left, right):
    return lax.dot_general(left, right, CONTRACT_LANES, preferred_element_type=F32)


def pack_kernel(*refs):
    sources, payload, held, sems = refs[:9], refs[9], refs[10:19], refs[19]
    copies = [pltpu.make_async_copy(a, b, sems.at[i]) for i, (a, b) in enumerate(zip(sources, held))]
    for copy in copies:
        copy.start()
    for copy in copies:
        copy.wait()
    residual, azimuth, elevation, brick, cell, force, px, py, pz = held
    cosine = jnp.cos(elevation[0])
    value = residual[0]
    gates, points = value.shape[1], px.shape[1]
    rest = jnp.zeros((1, gates - 2 * points), F32)
    rows = [
        cosine * jnp.cos(azimuth[0]) * value,
        cosine * jnp.sin(azimuth[0]) * value,
        jnp.sin(elevation[0]) * value,
        brick[...].astype(F32),
        cell[0].astype(F32),
        jnp.concatenate([force[0], force[1], force[2], px[...]], axis=1),
        jnp.concatenate([py[...], pz[...], rest], axis=1),
        jnp.zeros((1, gates), F32),
    ]
    for r, row in enumerate(rows):
        payload[r : r + 1, :] = row


def edges(sides, size_x):
    if sides == 1:
        return [jnp.where(lax.axis_index("stream") == 0, size_x - HALO, 0)]
    return [size_x - HALO, 0]


def lines_of(payload, spans, start_x, size_y, size_z):
    brick = payload[3:4, :].astype(jnp.int32)
    cell = payload[4:5, :].astype(jnp.int32)
    away = brick - lax.axis_index("span")
    away = jnp.where(away < 0, away + spans, away)
    x = cell // (size_y * size_z)
    y = cell // size_z % size_y
    upper = (away == 1) & (y < HALO)
    lower = (away == spans - 1) & (y >= size_y - HALO)
    row = jnp.where(away == 0, y, jnp.where(upper, y + size_y, jnp.where(lower, y + 2 * HALO, -1)))
    return jnp.where(row < 0, -1, (x - start_x) * (size_y + 2 * HALO) + row), cell % size_z


def spread(payload_of, spans, sources, near, out, start_x, planes, size_y, size_z, first, unroll=False):
    ext_y = size_y + 2 * HALO
    height = planes * ext_y
    points = payload_of(0).shape[1] // 4
    count = len(near) * points
    rows = [[payload_of(j)[r : r + 1, :] for r in (5, 6)] for j, _ in near]

    def joined(r, k):
        return jnp.concatenate([pair[r][:, k * points : (k + 1) * points] for pair in rows], axis=1)

    px, pz = joined(0, 3), joined(1, 1)
    py = jnp.concatenate(
        [pair[1][:, 0:points] + F32(side * size_y) for pair, (_, side) in zip(rows, near)], axis=1
    )
    y_row = lax.broadcasted_iota(jnp.int32, (ext_y, count), 0)
    by = bump(jnp.where(y_row < size_y + HALO, y_row, y_row - ext_y).astype(F32) - py)
    x_cell = (lax.broadcasted_iota(jnp.int32, (planes, count), 0) + start_x).astype(F32)
    bx = bump(x_cell - px)
    z_cell = lax.broadcasted_iota(jnp.int32, (size_z, count), 0) + lax.axis_index("vert") * size_z
    bz_high, bz_low = two_parts(bump(z_cell.astype(F32) - pz))
    cross = jnp.concatenate([by * bx[x : x + 1] for x in range(planes)], axis=0)
    parts = [two_parts(cross * joined(0, c)) for c in range(3)]
    by_high = dot_lanes(jnp.concatenate([part for pair in parts for part in pair], axis=0), bz_high)
    by_low = dot_lanes(jnp.concatenate([high for high, _ in parts], axis=0), bz_low)
    for c in range(3):
        high = 2 * c * height
        both = by_high[high : high + height] + by_high[high + height : high + 2 * height]
        both += by_low[c * height : (c + 1) * height]
        out[c] = both if first is None else first[c] + both

    gates = payload_of(0).shape[1]
    row_id = lax.broadcasted_iota(jnp.int32, (height, gates), 0)
    z_id = lax.broadcasted_iota(jnp.int32, (size_z, gates), 0)

    def one_source(j, carry):
        one = payload_of(j)
        line, z = lines_of(one, spans, start_x, size_y, size_z)
        pick = jnp.where(row_id == line, 1.0, 0.0).astype(BF16)
        pick_z = jnp.where(z_id == z, 1.0, 0.0).astype(BF16)
        parts = [part for c in range(3) for part in two_parts(one[c : c + 1, :])]
        sums = dot_lanes(jnp.concatenate([pick * part for part in parts], axis=0), pick_z)
        for c in range(3):
            high = 2 * c * height
            out[c] += sums[high : high + height] + sums[high + height : high + 2 * height]
        return carry

    if unroll:
        for j in range(*sources):
            one_source(j, 0)
    else:
        lax.fori_loop(*sources, one_source, 0)


def near_of(spans):
    return ((0, 0), (spans - 1, -1), (2 if spans == 4 else 1, 1))


def first_kernel(spans, dims, payload, out):
    size_x, size_y, size_z = dims
    spread(lambda j: payload, spans, (0, 1), near_of(spans)[:1], out, 0, size_x, size_y, size_z, None, unroll=True)


def payload_in(refs, j):
    return refs[0].at[j] if len(refs) == 1 else refs[j]


def second_kernel(spans, dims, count, *refs):
    payloads, (first, out) = refs[:count], refs[count:]
    size_x, size_y, size_z = dims
    near = near_of(spans)[1:]
    spread(lambda j: payload_in(payloads, j), spans, (1, spans), near, out, 0, size_x, size_y, size_z, first, unroll=count > 1)


def gather_kernel(spans, sides, count, *refs):
    payloads, (kappa, sigma, to_upper, to_lower), outs = refs[:count], refs[count : count + 4], refs[count + 4 :]
    size_x, size_y, size_z = kappa.shape
    for out, start in zip(outs, edges(sides, size_x)):
        each = payloads[0].shape[-1] // size_z
        for j in range(spans):
            one = payload_in(payloads, j)
            for part in range(each):
                out[j * each + part] = one[:, part * size_z : (part + 1) * size_z]
        for i in range(HALO):
            for k, field in enumerate((kappa, sigma)):
                plane = field[start + i]
                for part in range(size_y // 8):
                    out[spans * each + (2 * i + k) * (size_y // 8) + part] = plane[8 * part : 8 * part + 8]
    to_upper[:, 0:HALO] = kappa[:, size_y - HALO :]
    to_upper[:, HALO:] = sigma[:, size_y - HALO :]
    to_lower[:, 0:HALO] = kappa[:, 0:HALO]
    to_lower[:, HALO:] = sigma[:, 0:HALO]


def corner_kernel(sides, upper, lower, *outs):
    for out, start in zip(outs, edges(sides, upper.shape[0])):
        out[:, 0 : 2 * HALO] = upper[pl.ds(start, HALO)]
        out[:, 2 * HALO :] = lower[pl.ds(start, HALO)]


def strip_kernel(spans, sides, dims, *refs):
    size_x, size_y, size_z = dims
    starts = edges(sides, size_x)
    starts = [size_x - HALO - starts[0]] if sides == 1 else starts[::-1]
    for packed, strip, start in zip(refs[:sides], refs[sides:], starts):
        each = (packed.shape[0] - HALO * 2 * size_y // 8) // spans

        def payload_of(j, packed=packed, each=each):
            return jnp.concatenate([packed[j * each + part] for part in range(each)], axis=1)

        spread(payload_of, spans, (0, spans), near_of(spans), strip, start, HALO, size_y, size_z, None)


def extend_kernel(sides, *refs):
    own, kappa, sigma, upper, lower = refs[:5]
    strips, others, corners = (refs[5 + k * sides : 5 + (k + 1) * sides] for k in range(3))
    source, kappa_ext, face = refs[5 + 3 * sides :]
    size_x, size_y, size_z = kappa.shape
    ext_y = size_y + 2 * HALO
    vert = lax.axis_index("vert")
    side = pl.ds(pl.multiple_of(jnp.where(vert == 0, size_z - 128, 0), 128), 128)
    for x in range(size_x + sides * HALO):
        if x < size_x:
            kappa_ext[x] = jnp.concatenate([kappa[x], upper[x, 0:HALO], lower[x, 0:HALO]], axis=0)
            sig = jnp.concatenate([sigma[x], upper[x, HALO:], lower[x, HALO:]], axis=0)
        else:
            packed, corner = others[(x - size_x) // HALO], corners[(x - size_x) // HALO]
            i = (x - size_x) % HALO
            tiles = size_y // 8
            base = packed.shape[0] - (HALO - i) * 2 * tiles
            slab = [packed[base + k] for k in range(2 * tiles)]
            up, low = corner[i, 0 : 2 * HALO], corner[i, 2 * HALO :]
            kappa_ext[x] = jnp.concatenate([*slab[:tiles], up[0:HALO], low[0:HALO]], axis=0)
            sig = jnp.concatenate([*slab[tiles:], up[HALO:], low[HALO:]], axis=0)
        for c in range(3):
            if x < size_x:
                value = own[c, x * ext_y : (x + 1) * ext_y, :]
            else:
                place = (x - size_x) % HALO * ext_y
                value = strips[(x - size_x) // HALO][c, place : place + ext_y, :]
            source[c, x] = value * sig
    lane = lax.broadcasted_iota(jnp.int32, (8, 128), 1)
    tiles = face_tiles(size_x + sides * HALO, ext_y)
    for g in range(0, len(tiles), 16):
        packed = jnp.zeros((8, 128), F32)
        for k, (c, x, y) in enumerate(tiles[g : g + 16]):
            tile = kappa_ext[x, y : y + 8, side] if c == 3 else source[c, x, y : y + 8, side]
            turned = pltpu.roll(tile, (8 * k + 8 * (1 - vert)) & 127, 1)
            packed = jnp.where(lane // 8 == k, turned, packed)
        face[g // 16] = packed


def face_tiles(planes, ext_y):
    return [(c, x, y) for c in range(4) for x in range(planes) for y in range(0, ext_y, 8)]


def lanes_on(values, step, lane):
    tiles = [values[:, k : k + 128] for k in range(0, values.shape[1], 128)]
    turned = [pltpu.roll(tile, step % 128, 1) for tile in tiles]
    edge = lane == (0 if step == 1 else 127)
    return jnp.concatenate(
        [jnp.where(edge, turned[(k - step) % len(tiles)], turned[k]) for k in range(len(tiles))], axis=1
    )


def each_plane(count, step, unroll=4):
    whole = count // unroll * unroll
    lax.fori_loop(0, whole, lambda i, carry: (step(i), carry)[1], 0, unroll=unroll)
    for i in range(whole, count):
        step(i)


def coefficient_kernel(sides, size_x, kappa_ext, root, ax, ay, aym, az, azm, keep):
    planes, ext_y, size_z = kappa_ext.shape
    stream, last = lax.axis_index("stream"), lax.axis_size("stream") - 1
    place = lax.broadcasted_iota(jnp.int32, (ext_y, size_z), 1)
    lane = lax.broadcasted_iota(jnp.int32, (ext_y, 128), 1)

    def roots(x):
        root[x] = jnp.sqrt(kappa_ext[x])

    each_plane(planes, roots)

    def faces(x):
        after = jnp.where(x == planes - 1, 0, x + 1)
        here = root[x]
        wall = ((x == planes - 1) & (stream == 0)) | ((x == size_x - 1) & (stream == last))
        ax[x] = here * root[after] * jnp.where(wall, 0.0, 1.0)
        up = here * pltpu.roll(here, ext_y - 1, 0)
        ay[x] = up
        aym[x] = pltpu.roll(up, 1, 0)
        up = jnp.where(place == size_z - 1, 0.0, here * lanes_on(here, -1, lane))
        az[x] = up
        azm[x] = lanes_on(up, 1, lane)

    each_plane(planes, faces)

    def rest(x):
        before = jnp.where(x == 0, planes - 1, x - 1)
        keep[x] = 1.0 - (ax[x] + ax[before] + ay[x] + aym[x] + az[x] + azm[x])

    each_plane(planes, rest)


def diffuse_kernel(sides, source, root, ax, ay, aym, az, azm, keep, face, out, *scratch):
    ping, pong, halo, root_h, ax_h, ay_h, aym_h, az_all, azm_all, keep_all = scratch
    planes, ext_y, size_z = root.shape
    size_x, size_y = out.shape[1], out.shape[2]
    ext_z = size_z + 128
    stream, vert = lax.axis_index("stream"), lax.axis_index("vert")
    last = lax.axis_size("stream") - 1
    for x in range(size_x, planes):
        for c in range(3):
            ping[c, x] = jnp.zeros((ext_y, ext_z), F32)
            pong[c, x] = jnp.zeros((ext_y, ext_z), F32)
    lane = lax.broadcasted_iota(jnp.int32, (ext_y, 128), 1)
    known = lax.broadcasted_iota(jnp.int32, (8, 128), 1) // 8 == vert * 15
    for t, (c, x, y) in enumerate(face_tiles(planes, ext_y)):
        turned = pltpu.roll(face[t // 16], (256 - 8 * (t % 16) - 8 * vert) & 127, 1)
        if c == 3:
            root_h[x, y : y + 8, :] = jnp.sqrt(jnp.where(known, turned, 0.0))
        else:
            halo[c, x, y : y + 8, :] = turned

    def faces(x):
        after = jnp.where(x == planes - 1, 0, x + 1)
        here, low, high = root_h[x], root[x, :, 0:128], root[x, :, size_z - 128 :]
        wall = ((x == planes - 1) & (stream == 0)) | ((x == size_x - 1) & (stream == last))
        ax_h[x] = here * root_h[after] * jnp.where(wall, 0.0, 1.0)
        up = here * pltpu.roll(here, ext_y - 1, 0)
        ay_h[x] = up
        aym_h[x] = pltpu.roll(up, 1, 0)
        over, under = pltpu.roll(here, 127, 1), pltpu.roll(here, 1, 1)
        az_h = here * jnp.where(lane == 127, pltpu.roll(low, 127, 1), over)
        azm_h = here * jnp.where(lane == 0, pltpu.roll(high, 1, 1), under)
        top = jnp.where(lane == 127, high * over, 0.0)
        bottom = jnp.where(lane == 0, low * under, 0.0)
        none = [jnp.zeros((ext_y, 128), F32)] * (size_z // 128 - 1)
        top, bottom = jnp.concatenate([*none, top], axis=1), jnp.concatenate([bottom, *none], axis=1)
        az_all[x, :, 0:size_z] = az[x] + top
        az_all[x, :, size_z:] = az_h
        azm_all[x, :, 0:size_z] = azm[x] + bottom
        azm_all[x, :, size_z:] = azm_h
        keep_all[x, :, 0:size_z] = keep[x] - (top + bottom)

    each_plane(planes, faces)

    def rest(x):
        before = jnp.where(x == 0, planes - 1, x - 1)
        sides_sum = ax_h[x] + ax_h[before] + ay_h[x] + aym_h[x]
        keep_all[x, :, size_z:] = 1.0 - (sides_sum + az_all[x, :, size_z:] + azm_all[x, :, size_z:])

    each_plane(planes, rest)

    def wide(main, beside):
        return jnp.concatenate([main, beside], axis=1)

    for p in range(PASSES):
        deep = PASSES - 1 - p
        old, new = (ping, pong) if p % 2 == 0 else (pong, ping)
        first = jnp.where(stream == 0, 0, planes - deep) if sides == 1 else planes - deep

        def value_of(c, x, old=old, p=p):
            return wide(source[c, x], halo[c, x]) if p == 0 else old[c, x]

        def one_plane(i, value_of=value_of, new=new, first=first, p=p):
            x = i + first
            x = jnp.where(x >= planes, x - planes, x)
            after = jnp.where(x == planes - 1, 0, x + 1)
            before = jnp.where(x == 0, planes - 1, x - 1)
            for c in range(3):
                value = value_of(c, x)
                moved = keep_all[x] * value
                moved += wide(ax[x], ax_h[x]) * value_of(c, after) + wide(ax[before], ax_h[before]) * value_of(c, before)
                moved += wide(ay[x], ay_h[x]) * pltpu.roll(value, ext_y - 1, 0)
                moved += wide(aym[x], aym_h[x]) * pltpu.roll(value, 1, 0)
                moved += az_all[x] * lanes_on(value, -1, lane) + azm_all[x] * lanes_on(value, 1, lane)
                if p == PASSES - 1:
                    out[c, x] = moved[0:size_y, 0:size_z]
                else:
                    new[c, x] = moved

        each_plane(size_x + sides * deep, one_plane)


def call(kernel, outs, scratch, flops, *args, left=(), aliases=(), room=8):
    moved = sum(4 * a.size for a in args) + sum(4 * o.size for o in outs)
    spaces = [pltpu.HBM if i in left else pltpu.VMEM for i in range(len(args))]
    return pl.pallas_call(
        kernel,
        out_shape=outs,
        in_specs=[pl.BlockSpec(memory_space=space) for space in spaces],
        out_specs=[pl.BlockSpec(memory_space=pltpu.VMEM)] * len(outs),
        scratch_shapes=scratch,
        input_output_aliases=dict(aliases),
        compiler_params=pltpu.CompilerParams(vmem_limit_bytes=room * 1024 * 1024),
        cost_estimate=pl.CostEstimate(flops=flops, bytes_accessed=moved, transcendentals=0),
    )(*args)


def ring(array, step):
    count = lax.axis_size("span")
    return lax.ppermute(array, "span", [(i, (i + step) % count) for i in range(count)])


def across_bands(arrays):
    count = lax.axis_size("stream")
    if count == 2:
        return [lax.ppermute(arrays[0], "stream", [(0, 1), (1, 0)])]
    return [
        lax.ppermute(arrays[1], "stream", [(i + 1, i) for i in range(count - 1)]),
        lax.ppermute(arrays[0], "stream", [(i, i + 1) for i in range(count - 1)]),
    ]


def on_device(
    kappa,
    sigma,
    gate_residual,
    gate_azimuth,
    gate_elevation,
    gate_brick,
    gate_cell,
    blade_force,
    point_x,
    point_y,
    point_z,
):
    size_x, size_y, size_z = kappa.shape
    spans = lax.axis_size("span")
    sides = 1 if lax.axis_size("stream") == 2 else 2
    gates = gate_residual.shape[2]
    ext_x, ext_y = size_x + sides * HALO, size_y + 2 * HALO
    shape = lambda *dims: jax.ShapeDtypeStruct(dims, F32)
    inputs = [
        gate_residual,
        gate_azimuth,
        gate_elevation,
        gate_brick.reshape(1, gates),
        gate_cell,
        blade_force,
        point_x,
        point_y,
        point_z,
    ]
    (payload,) = call(
        pack_kernel,
        [shape(8, gates)],
        [pltpu.VMEM(a.shape, a.dtype) for a in inputs] + [pltpu.SemaphoreType.DMA((len(inputs),))],
        1000,
        *[pltpu.with_memory_space_constraint(a, pltpu.HBM) for a in inputs],
        left=range(len(inputs)),
    )
    if spans == 4:
        payloads = [payload, ring(payload, 2), ring(payload, -1), ring(payload, 1)]
    else:
        payloads = [jnp.roll(lax.all_gather(payload, "span"), -lax.axis_index("span"), axis=0)]
    dims = (size_x, size_y, size_z)
    work = 12 * size_x * ext_y * size_z * gates
    planes = shape(3, size_x * ext_y, size_z)
    (own,) = call(functools.partial(first_kernel, spans, dims), [planes], [], work, payload, room=24)
    parts = spans * gates // size_z + HALO * 2 * size_y // 8
    to_upper, to_lower, *others = call(
        functools.partial(gather_kernel, spans, sides, len(payloads)),
        [shape(size_x, 2 * HALO, size_z)] * 2 + [shape(parts, 8, size_z)] * sides,
        [],
        1000,
        *payloads,
        kappa,
        sigma,
    )
    others = across_bands(others)
    from_lower, from_upper = ring(to_upper, 1), ring(to_lower, -1)
    (own,) = call(
        functools.partial(second_kernel, spans, dims, len(payloads)),
        [planes],
        [],
        work * (spans - 1),
        *payloads,
        own,
        aliases=((len(payloads), 0),),
        room=24,
    )
    corners = across_bands(
        call(
            functools.partial(corner_kernel, sides),
            [shape(HALO, 4 * HALO, size_z)] * sides,
            [],
            1000,
            from_upper,
            from_lower,
        )
    )
    strips = call(
        functools.partial(strip_kernel, spans, sides, dims),
        [shape(3, HALO * ext_y, size_z)] * sides,
        [],
        work // 4 * spans,
        *others,
        room=24,
    )
    tiles = len(face_tiles(ext_x, ext_y))
    source, kappa_ext, face = call(
        functools.partial(extend_kernel, sides),
        [shape(3, ext_x, ext_y, size_z), shape(ext_x, ext_y, size_z), shape(-(-tiles // 16), 8, 128)],
        [],
        1000,
        own,
        kappa,
        sigma,
        from_upper,
        from_lower,
        *strips,
        *others,
        *corners,
    )
    face = lax.ppermute(face, "vert", [(0, 1), (1, 0)])
    main, beside, wide = ((ext_x, ext_y, width) for width in (size_z, 128, size_z + 128))
    coefficients = call(
        functools.partial(coefficient_kernel, sides, size_x), [shape(*main)] * 7, [], 30 * ext_x * ext_y * size_z, kappa_ext
    )
    scratch = [(3, *wide)] * 2 + [(3, *beside)] + [beside] * 4 + [wide] * 3
    (field,) = call(
        functools.partial(diffuse_kernel, sides),
        [shape(3, size_x, size_y, size_z)],
        [pltpu.VMEM(dims, F32) for dims in scratch],
        60 * 3 * ext_x * ext_y * size_z,
        source,
        *coefficients,
        face,
        room=20,
    )
    return field


def solution(mesh):
    placed = (
        P(("grp", "stream"), "span", "vert"),
        P(("grp", "stream"), "span", "vert"),
        P(("grp", "stream"), "vert", "span"),
        P(("grp", "stream"), "vert", "span"),
        P(("grp", "stream"), "vert", "span"),
        P(("grp", "stream"), "vert", "span", None),
        P(("grp", "stream"), "vert", "span"),
        P(None, ("grp", "stream"), "span"),
        P(("grp", "stream"), "span"),
        P(("grp", "stream"), "span"),
        P(("grp", "stream"), "span"),
    )
    return jax.shard_map(
        on_device,
        mesh=mesh,
        in_specs=placed,
        out_specs=P(None, ("grp", "stream"), "span", "vert"),
        check_vma=False,
    )
```

```python
import functools

import jax
import jax.numpy as jnp
from jax import lax
from jax.experimental import pallas as pl
from jax.experimental.pallas import tpu as pltpu
from jax.sharding import PartitionSpec as P

SPREAD = 6
PASSES = 4
HALO = 4
BF16 = jnp.bfloat16
F32 = jnp.float32
F8 = jnp.float8_e4m3fn
CONTRACT_LANES = (((1,), (1,)), ((), ()))


def bump(distance):
    scaled = distance * F32(1.0 / SPREAD)
    return jnp.square(jnp.maximum(0.0, 1.0 - scaled * scaled))


def two_parts(values):
    high = values.astype(BF16)
    return high, (values - high.astype(F32)).astype(BF16)


def dot_lanes(left, right):
    return lax.dot_general(left, right, CONTRACT_LANES, preferred_element_type=F32)


def pack_kernel(*refs):
    sources, (payload, *fields), held, sems = refs[:11], refs[11:14], refs[14:23], refs[23]
    copies = [pltpu.make_async_copy(a, b, sems.at[i]) for i, (a, b) in enumerate(zip(sources[:9], held))]
    pieces = (sems.shape[0] - 9) // 2
    step = fields[0].shape[0] // pieces
    slow = [
        pltpu.make_async_copy(
            a.at[pl.ds(k * step, step)], b.at[pl.ds(k * step, step)], sems.at[9 + n * pieces + k]
        )
        for n, (a, b) in enumerate(zip(sources[9:], fields))
        for k in range(pieces)
    ]
    for copy in copies + slow:
        copy.start()
    for copy in copies:
        copy.wait()
    residual, azimuth, elevation, brick, cell, force, px, py, pz = held
    cosine = jnp.cos(elevation[0])
    value = residual[0]
    gates, points = value.shape[1], px.shape[1]
    rest = jnp.zeros((1, gates - 2 * points), F32)
    rows = [
        cosine * jnp.cos(azimuth[0]) * value,
        cosine * jnp.sin(azimuth[0]) * value,
        jnp.sin(elevation[0]) * value,
        brick[...].astype(F32),
        cell[0].astype(F32),
        jnp.concatenate([force[0], force[1], force[2], px[...]], axis=1),
        jnp.concatenate([py[...], pz[...], rest], axis=1),
        jnp.zeros((1, gates), F32),
    ]
    for r, row in enumerate(rows):
        payload[r : r + 1, :] = row
    for copy in slow:
        copy.wait()


def edges(sides, size_x):
    if sides == 1:
        return [jnp.where(lax.axis_index("stream") == 0, size_x - HALO, 0)]
    return [size_x - HALO, 0]


def lines_of(payload, spans, start_x, size_y, size_z):
    brick = payload[3:4, :].astype(jnp.int32)
    cell = payload[4:5, :].astype(jnp.int32)
    away = brick - lax.axis_index("span")
    away = jnp.where(away < 0, away + spans, away)
    x = cell // (size_y * size_z)
    y = cell // size_z % size_y
    upper = (away == 1) & (y < HALO)
    lower = (away == spans - 1) & (y >= size_y - HALO)
    row = jnp.where(away == 0, y, jnp.where(upper, y + size_y, jnp.where(lower, y + 2 * HALO, -1)))
    return jnp.where(row < 0, -1, (x - start_x) * (size_y + 2 * HALO) + row), cell % size_z


def spread_points(payload_of, near, out, start_x, planes, size_y, size_z, first):
    ext_y = size_y + 2 * HALO
    height = planes * ext_y
    points = payload_of(0).shape[1] // 4
    count = len(near) * points
    rows = [[payload_of(j)[r : r + 1, :] for r in (5, 6)] for j, _ in near]

    def joined(r, k):
        return jnp.concatenate([pair[r][:, k * points : (k + 1) * points] for pair in rows], axis=1)

    px, pz = joined(0, 3), joined(1, 1)
    py = jnp.concatenate(
        [pair[1][:, 0:points] + F32(side * size_y) for pair, (_, side) in zip(rows, near)], axis=1
    )
    y_row = lax.broadcasted_iota(jnp.int32, (ext_y, count), 0)
    by = bump(jnp.where(y_row < size_y + HALO, y_row, y_row - ext_y).astype(F32) - py)
    x_cell = (lax.broadcasted_iota(jnp.int32, (planes, count), 0) + start_x).astype(F32)
    bx = bump(x_cell - px)
    z_cell = lax.broadcasted_iota(jnp.int32, (size_z, count), 0) + lax.axis_index("vert") * size_z
    bz_high, bz_low = two_parts(bump(z_cell.astype(F32) - pz))
    cross = jnp.concatenate([by * bx[x : x + 1] for x in range(planes)], axis=0)
    parts = [two_parts(cross * joined(0, c)) for c in range(3)]
    by_high = dot_lanes(jnp.concatenate([part for pair in parts for part in pair], axis=0), bz_high)
    by_low = dot_lanes(jnp.concatenate([high for high, _ in parts], axis=0), bz_low)
    for c in range(3):
        high = 2 * c * height
        both = by_high[high : high + height] + by_high[high + height : high + 2 * height]
        both += by_low[c * height : (c + 1) * height]
        out[c] = both if first is None else first[c] + both


def spread_gates(payload_of, spans, sources, out, start_x, planes, size_y, size_z, unroll=False):
    height = planes * (size_y + 2 * HALO)
    gates = payload_of(0).shape[1]
    row_id = lax.broadcasted_iota(jnp.int32, (height, gates), 0)
    z_id = lax.broadcasted_iota(jnp.int32, (size_z, gates), 0)

    def one_source(j, carry):
        one = payload_of(j)
        line, z = lines_of(one, spans, start_x, size_y, size_z)
        pick = jnp.where(row_id == line, 1.0, 0.0).astype(BF16)
        there = jnp.where(z_id == z, 1.0, 0.0).astype(BF16)
        high, low = zip(*[two_parts(one[c : c + 1, :]) for c in range(3)])
        if height <= 128:
            sums = dot_lanes(jnp.concatenate([pick * part for part in high + low], axis=0), there)
            for c in range(3):
                more = sums[(c + 3) * height : (c + 4) * height]
                out[c] += sums[c * height : (c + 1) * height] + more
            return carry
        scale = [256.0 / jnp.maximum(jnp.max(jnp.abs(part.astype(F32)), axis=1, keepdims=True), 1e-30) for part in low]
        low = [(pick * (part.astype(F32) * by).astype(BF16)).astype(F8) for part, by in zip(low, scale)]
        sums = dot_lanes(jnp.concatenate([pick * part for part in high], axis=0), there)
        rest = dot_lanes(jnp.concatenate(low, axis=0), there.astype(F8))
        for c in range(3):
            lines = slice(c * height, (c + 1) * height)
            out[c] += sums[lines] + rest[lines] * (1.0 / scale[c])
        return carry

    if unroll:
        for j in range(*sources):
            one_source(j, 0)
    else:
        lax.fori_loop(*sources, one_source, 0)


def near_of(spans):
    return ((0, 0), (spans - 1, -1), (2 if spans == 4 else 1, 1))


def first_kernel(spans, dims, payload, out):
    size_x, size_y, size_z = dims
    spread_points(lambda j: payload, near_of(spans)[:1], out, 0, size_x, size_y, size_z, None)
    spread_gates(lambda j: payload, spans, (0, 1), out, 0, size_x, size_y, size_z, unroll=True)


def payload_in(refs, j):
    return refs[0].at[j] if len(refs) == 1 else refs[j]


def second_kernel(spans, dims, count, *refs):
    payloads, (first, out) = refs[:count], refs[count:]
    for c in range(3):
        out[c] = first[c]
    spread_gates(lambda j: payload_in(payloads, j), spans, (1, spans), out, 0, *dims, unroll=count > 1)


def third_kernel(spans, dims, count, *refs):
    payloads, second, out = refs[:count], refs[count], refs[-1]
    spread_points(lambda j: payload_in(payloads, j), near_of(spans)[1:], out, 0, *dims, second)


def gather_kernel(spans, sides, count, *refs):
    payloads, (kappa, sigma), outs = refs[:count], refs[count : count + 2], refs[count + 2 :]
    size_x, size_y, size_z = kappa.shape
    for out, start in zip(outs, edges(sides, size_x)):
        each = payloads[0].shape[-1] // size_z
        for j in range(spans):
            one = payload_in(payloads, j)
            for part in range(each):
                out[j * each + part] = one[:, part * size_z : (part + 1) * size_z]
        for i in range(HALO):
            for k, field in enumerate((kappa, sigma)):
                plane = field[start + i]
                for part in range(size_y // 8):
                    out[spans * each + (2 * i + k) * (size_y // 8) + part] = plane[8 * part : 8 * part + 8]

def slab_kernel(kappa, sigma, to_upper, to_lower):
    size_y = kappa.shape[1]
    to_upper[:, 0:HALO] = kappa[:, size_y - HALO :]
    to_upper[:, HALO:] = sigma[:, size_y - HALO :]
    to_lower[:, 0:HALO] = kappa[:, 0:HALO]
    to_lower[:, HALO:] = sigma[:, 0:HALO]


def corner_kernel(sides, upper, lower, *outs):
    for out, start in zip(outs, edges(sides, upper.shape[0])):
        out[:, 0 : 2 * HALO] = upper[pl.ds(start, HALO)]
        out[:, 2 * HALO :] = lower[pl.ds(start, HALO)]


def strip_kernel(spans, sides, dims, *refs):
    size_x, size_y, size_z = dims
    starts = edges(sides, size_x)
    starts = [size_x - HALO - starts[0]] if sides == 1 else starts[::-1]
    for packed, strip, start in zip(refs[:sides], refs[sides:], starts):
        each = (packed.shape[0] - HALO * 2 * size_y // 8) // spans

        def payload_of(j, packed=packed, each=each):
            return jnp.concatenate([packed[j * each + part] for part in range(each)], axis=1)

        spread_points(payload_of, near_of(spans), strip, start, HALO, size_y, size_z, None)
        spread_gates(payload_of, spans, (0, spans), strip, start, HALO, size_y, size_z, unroll=spans == 4)


def extend_kernel(sides, *refs):
    own, kappa, sigma, upper, lower = refs[:5]
    strips, others, corners = (refs[5 + k * sides : 5 + (k + 1) * sides] for k in range(3))
    source, kappa_ext, face = refs[5 + 3 * sides :]
    size_x, size_y, size_z = kappa.shape
    ext_y = size_y + 2 * HALO
    vert = lax.axis_index("vert")
    side = pl.ds(pl.multiple_of(jnp.where(vert == 0, size_z - 128, 0), 128), 128)
    for x in range(size_x + sides * HALO):
        if x < size_x:
            kappa_ext[x] = jnp.concatenate([kappa[x], upper[x, 0:HALO], lower[x, 0:HALO]], axis=0)
            sig = jnp.concatenate([sigma[x], upper[x, HALO:], lower[x, HALO:]], axis=0)
        else:
            packed, corner = others[(x - size_x) // HALO], corners[(x - size_x) // HALO]
            i = (x - size_x) % HALO
            tiles = size_y // 8
            base = packed.shape[0] - (HALO - i) * 2 * tiles
            slab = [packed[base + k] for k in range(2 * tiles)]
            up, low = corner[i, 0 : 2 * HALO], corner[i, 2 * HALO :]
            kappa_ext[x] = jnp.concatenate([*slab[:tiles], up[0:HALO], low[0:HALO]], axis=0)
            sig = jnp.concatenate([*slab[tiles:], up[HALO:], low[HALO:]], axis=0)
        for c in range(3):
            if x < size_x:
                value = own[c, x * ext_y : (x + 1) * ext_y, :]
            else:
                place = (x - size_x) % HALO * ext_y
                value = strips[(x - size_x) // HALO][c, place : place + ext_y, :]
            source[c, x] = value * sig
    lane = lax.broadcasted_iota(jnp.int32, (8, 128), 1)
    tiles = face_tiles(size_x + sides * HALO, ext_y)
    for g in range(0, len(tiles), 16):
        packed = jnp.zeros((8, 128), F32)
        for k, (c, x, y) in enumerate(tiles[g : g + 16]):
            tile = kappa_ext[x, y : y + 8, side] if c == 3 else source[c, x, y : y + 8, side]
            turned = pltpu.roll(tile, (8 * k + 8 * (1 - vert)) & 127, 1)
            packed = jnp.where(lane // 8 == k, turned, packed)
        face[g // 16] = packed


def face_tiles(planes, ext_y):
    return [(c, x, y) for c in range(4) for x in range(planes) for y in range(0, ext_y, 8)]


def lanes_on(values, step, lane):
    tiles = [values[:, k : k + 128] for k in range(0, values.shape[1], 128)]
    turned = [pltpu.roll(tile, step % 128, 1) for tile in tiles]
    edge = lane == (0 if step == 1 else 127)
    return jnp.concatenate(
        [jnp.where(edge, turned[(k - step) % len(tiles)], turned[k]) for k in range(len(tiles))], axis=1
    )


def each_plane(count, step, unroll=8):
    whole = count // unroll * unroll
    lax.fori_loop(0, whole, lambda i, carry: (step(i), carry)[1], 0, unroll=unroll)
    for i in range(whole, count):
        step(i)


def coefficient_kernel(sides, size_x, kappa_ext, root, ax, ay, aym, az, azm, keep):
    planes, ext_y, size_z = kappa_ext.shape
    stream, last = lax.axis_index("stream"), lax.axis_size("stream") - 1
    place = lax.broadcasted_iota(jnp.int32, (ext_y, size_z), 1)
    lane = lax.broadcasted_iota(jnp.int32, (ext_y, 128), 1)

    def roots(x):
        root[x] = jnp.sqrt(kappa_ext[x])

    each_plane(planes, roots)

    def faces(x):
        after = jnp.where(x == planes - 1, 0, x + 1)
        here = root[x]
        wall = ((x == planes - 1) & (stream == 0)) | ((x == size_x - 1) & (stream == last))
        ax[x] = here * root[after] * jnp.where(wall, 0.0, 1.0)
        up = here * pltpu.roll(here, ext_y - 1, 0)
        ay[x] = up
        aym[x] = pltpu.roll(up, 1, 0)
        up = jnp.where(place == size_z - 1, 0.0, here * lanes_on(here, -1, lane))
        az[x] = up
        azm[x] = lanes_on(up, 1, lane)

    each_plane(planes, faces)

    def rest(x):
        before = jnp.where(x == 0, planes - 1, x - 1)
        keep[x] = 1.0 - (ax[x] + ax[before] + ay[x] + aym[x] + az[x] + azm[x])

    each_plane(planes, rest)


def diffuse_kernel(sides, source, root, ax, ay, aym, az, azm, keep, face, out, *scratch):
    ping, pong, halo, root_h, ax_h, ay_h, aym_h, az_all, azm_all, keep_all, done, sems = scratch
    planes, ext_y, size_z = root.shape
    size_x, size_y = out.shape[1], out.shape[2]
    ext_z = size_z + 128
    stream, vert = lax.axis_index("stream"), lax.axis_index("vert")
    last = lax.axis_size("stream") - 1
    for x in range(size_x, planes):
        for c in range(3):
            ping[c, x] = jnp.zeros((ext_y, ext_z), F32)
            pong[c, x] = jnp.zeros((ext_y, ext_z), F32)
    lane = lax.broadcasted_iota(jnp.int32, (ext_y, 128), 1)
    known = lax.broadcasted_iota(jnp.int32, (8, 128), 1) // 8 == vert * 15
    for t, (c, x, y) in enumerate(face_tiles(planes, ext_y)):
        turned = pltpu.roll(face[t // 16], (256 - 8 * (t % 16) - 8 * vert) & 127, 1)
        if c == 3:
            root_h[x, y : y + 8, :] = jnp.sqrt(jnp.where(known, turned, 0.0))
        else:
            halo[c, x, y : y + 8, :] = turned

    def faces(x):
        after = jnp.where(x == planes - 1, 0, x + 1)
        here, low, high = root_h[x], root[x, :, 0:128], root[x, :, size_z - 128 :]
        wall = ((x == planes - 1) & (stream == 0)) | ((x == size_x - 1) & (stream == last))
        ax_h[x] = here * root_h[after] * jnp.where(wall, 0.0, 1.0)
        up = here * pltpu.roll(here, ext_y - 1, 0)
        ay_h[x] = up
        aym_h[x] = pltpu.roll(up, 1, 0)
        over, under = pltpu.roll(here, 127, 1), pltpu.roll(here, 1, 1)
        az_h = here * jnp.where(lane == 127, pltpu.roll(low, 127, 1), over)
        azm_h = here * jnp.where(lane == 0, pltpu.roll(high, 1, 1), under)
        top = jnp.where(lane == 127, high * over, 0.0)
        bottom = jnp.where(lane == 0, low * under, 0.0)
        none = [jnp.zeros((ext_y, 128), F32)] * (size_z // 128 - 1)
        top, bottom = jnp.concatenate([*none, top], axis=1), jnp.concatenate([bottom, *none], axis=1)
        az_all[x, :, 0:size_z] = az[x] + top
        az_all[x, :, size_z:] = az_h
        azm_all[x, :, 0:size_z] = azm[x] + bottom
        azm_all[x, :, size_z:] = azm_h
        keep_all[x, :, 0:size_z] = keep[x] - (top + bottom)

    each_plane(planes, faces)

    def rest(x):
        before = jnp.where(x == 0, planes - 1, x - 1)
        sides_sum = ax_h[x] + ax_h[before] + ay_h[x] + aym_h[x]
        keep_all[x, :, size_z:] = 1.0 - (sides_sum + az_all[x, :, size_z:] + azm_all[x, :, size_z:])

    each_plane(planes, rest)

    def wide(main, beside):
        return jnp.concatenate([main, beside], axis=1)

    for p in range(PASSES):
        deep = PASSES - 1 - p
        old, new = (ping, pong) if p % 2 == 0 else (pong, ping)
        first = (jnp.where(stream == 0, 0, planes - deep) if sides == 1 else planes - deep) if deep else 0

        def value_of(c, x, old=old, p=p):
            return wide(source[c, x], halo[c, x]) if p == 0 else old[c, x]

        def one_plane(i, value_of=value_of, new=new, first=first, p=p):
            x = i + first
            x = jnp.where(x >= planes, x - planes, x)
            after = jnp.where(x == planes - 1, 0, x + 1)
            before = jnp.where(x == 0, planes - 1, x - 1)
            for c in range(3):
                value = value_of(c, x)
                moved = keep_all[x] * value
                moved += wide(ax[x], ax_h[x]) * value_of(c, after) + wide(ax[before], ax_h[before]) * value_of(c, before)
                moved += wide(ay[x], ay_h[x]) * pltpu.roll(value, ext_y - 1, 0)
                moved += wide(aym[x], aym_h[x]) * pltpu.roll(value, 1, 0)
                moved += az_all[x] * lanes_on(value, -1, lane) + azm_all[x] * lanes_on(value, 1, lane)
                if p == PASSES - 1:
                    done[c, x] = moved[0:size_y, 0:size_z]
                else:
                    new[c, x] = moved

        if p < PASSES - 1:
            each_plane(size_x + sides * deep, one_plane)
    step = size_x // sems.shape[0]
    copies = []
    for k in range(sems.shape[0]):
        each_plane(step, lambda i, k=k: one_plane(i + k * step))
        part = pl.ds(k * step, step)
        copies.append(pltpu.make_async_copy(done.at[:, part], out.at[:, part], sems.at[k]))
        copies[-1].start()
    for copy in copies:
        copy.wait()


def call(kernel, outs, scratch, flops, *args, left=(), aliases=(), room=8, far=False):
    moved = sum(4 * a.size for a in args) + sum(4 * o.size for o in outs)
    spaces = [pltpu.HBM if i in left else pltpu.VMEM for i in range(len(args))]
    return pl.pallas_call(
        kernel,
        out_shape=outs,
        in_specs=[pl.BlockSpec(memory_space=space) for space in spaces],
        out_specs=[pl.BlockSpec(memory_space=pltpu.HBM if far else pltpu.VMEM)] * len(outs),
        scratch_shapes=scratch,
        input_output_aliases=dict(aliases),
        compiler_params=pltpu.CompilerParams(vmem_limit_bytes=room * 1024 * 1024),
        cost_estimate=pl.CostEstimate(flops=flops, bytes_accessed=moved, transcendentals=0),
    )(*args)


def ring(array, step):
    count = lax.axis_size("span")
    return lax.ppermute(array, "span", [(i, (i + step) % count) for i in range(count)])


def across_bands(arrays):
    count = lax.axis_size("stream")
    if count == 2:
        return [lax.ppermute(arrays[0], "stream", [(0, 1), (1, 0)])]
    return [
        lax.ppermute(arrays[1], "stream", [(i + 1, i) for i in range(count - 1)]),
        lax.ppermute(arrays[0], "stream", [(i, i + 1) for i in range(count - 1)]),
    ]


def on_device(
    kappa,
    sigma,
    gate_residual,
    gate_azimuth,
    gate_elevation,
    gate_brick,
    gate_cell,
    blade_force,
    point_x,
    point_y,
    point_z,
):
    size_x, size_y, size_z = kappa.shape
    spans = lax.axis_size("span")
    sides = 1 if lax.axis_size("stream") == 2 else 2
    gates = gate_residual.shape[2]
    ext_x, ext_y = size_x + sides * HALO, size_y + 2 * HALO
    shape = lambda *dims: jax.ShapeDtypeStruct(dims, F32)
    inputs = [
        gate_residual,
        gate_azimuth,
        gate_elevation,
        gate_brick.reshape(1, gates),
        gate_cell,
        blade_force,
        point_x,
        point_y,
        point_z,
        kappa,
        sigma,
    ]
    payload, kappa, sigma = call(
        pack_kernel,
        [shape(8, gates)] + [shape(size_x, size_y, size_z)] * 2,
        [pltpu.VMEM(a.shape, a.dtype) for a in inputs[:9]] + [pltpu.SemaphoreType.DMA((9 + 2 * 4,))],
        1000,
        *[pltpu.with_memory_space_constraint(a, pltpu.HBM) for a in inputs],
        left=range(len(inputs)),
    )
    if spans == 4:
        payloads = [payload, ring(payload, 2), ring(payload, -1), ring(payload, 1)]
    else:
        payloads = [jnp.roll(lax.all_gather(payload, "span"), -lax.axis_index("span"), axis=0)]
    dims = (size_x, size_y, size_z)
    work = 12 * size_x * ext_y * size_z * gates
    planes = shape(3, size_x * ext_y, size_z)
    (own,) = call(functools.partial(first_kernel, spans, dims), [planes], [], work, payload, room=24)
    parts = spans * gates // size_z + HALO * 2 * size_y // 8
    to_upper, to_lower = call(slab_kernel, [shape(size_x, 2 * HALO, size_z)] * 2, [], 1000, kappa, sigma)
    others = call(
        functools.partial(gather_kernel, spans, sides, len(payloads)),
        [shape(parts, 8, size_z)] * sides,
        [],
        1000,
        *payloads,
        kappa,
        sigma,
    )
    others = across_bands(others)
    from_lower, from_upper = ring(to_upper, 1), ring(to_lower, -1)
    (own,) = call(
        functools.partial(second_kernel, spans, dims, len(payloads)),
        [planes],
        [],
        work * (spans - 1),
        *payloads,
        own,
        aliases=((len(payloads), 0),),
        room=24,
    )
    corners = call(
        functools.partial(corner_kernel, sides),
        [shape(HALO, 4 * HALO, size_z)] * sides,
        [],
        1000,
        from_upper,
        from_lower,
    )
    (own,) = call(
        functools.partial(third_kernel, spans, dims, len(payloads)),
        [planes],
        [],
        work // 4,
        *payloads,
        own,
        *corners,
        aliases=((len(payloads), 0),),
        room=24,
    )
    corners = across_bands(corners)
    strips = call(
        functools.partial(strip_kernel, spans, sides, dims),
        [shape(3, HALO * ext_y, size_z)] * sides,
        [],
        work // 4 * spans,
        *others,
        room=24,
    )
    tiles = len(face_tiles(ext_x, ext_y))
    source, kappa_ext, face = call(
        functools.partial(extend_kernel, sides),
        [shape(3, ext_x, ext_y, size_z), shape(ext_x, ext_y, size_z), shape(-(-tiles // 16), 8, 128)],
        [],
        1000,
        own,
        kappa,
        sigma,
        from_upper,
        from_lower,
        *strips,
        *others,
        *corners,
    )
    face = lax.ppermute(face, "vert", [(0, 1), (1, 0)])
    main, beside, wide = ((ext_x, ext_y, width) for width in (size_z, 128, size_z + 128))
    coefficients = call(
        functools.partial(coefficient_kernel, sides, size_x), [shape(*main)] * 7, [], 30 * ext_x * ext_y * size_z, kappa_ext
    )
    scratch = [(3, *wide)] * 2 + [(3, *beside)] + [beside] * 4 + [wide] * 3 + [(3, size_x, size_y, size_z)]
    (field,) = call(
        functools.partial(diffuse_kernel, sides),
        [shape(3, size_x, size_y, size_z)],
        [pltpu.VMEM(dims, F32) for dims in scratch] + [pltpu.SemaphoreType.DMA((4,))],
        60 * 3 * ext_x * ext_y * size_z,
        source,
        *coefficients,
        face,
        room=20,
        far=True,
    )
    return field


def solution(mesh):
    placed = (
        P(("grp", "stream"), "span", "vert"),
        P(("grp", "stream"), "span", "vert"),
        P(("grp", "stream"), "vert", "span"),
        P(("grp", "stream"), "vert", "span"),
        P(("grp", "stream"), "vert", "span"),
        P(("grp", "stream"), "vert", "span", None),
        P(("grp", "stream"), "vert", "span"),
        P(None, ("grp", "stream"), "span"),
        P(("grp", "stream"), "span"),
        P(("grp", "stream"), "span"),
        P(("grp", "stream"), "span"),
    )
    return jax.shard_map(
        on_device,
        mesh=mesh,
        in_specs=placed,
        out_specs=P(None, ("grp", "stream"), "span", "vert"),
        check_vma=False,
    )
```

```python
import functools

import jax
import jax.numpy as jnp
from jax import lax
from jax.experimental import pallas as pl
from jax.experimental.pallas import tpu as pltpu
from jax.sharding import PartitionSpec as P

SPREAD = 6
PASSES = 4
HALO = 4
BF16 = jnp.bfloat16
F32 = jnp.float32
F8 = jnp.float8_e4m3fn
CONTRACT_LANES = (((1,), (1,)), ((), ()))


def bump(distance):
    scaled = distance * F32(1.0 / SPREAD)
    return jnp.square(jnp.maximum(0.0, 1.0 - scaled * scaled))


def two_parts(values):
    high = values.astype(BF16)
    return high, (values - high.astype(F32)).astype(BF16)


def dot_lanes(left, right):
    return lax.dot_general(left, right, CONTRACT_LANES, preferred_element_type=F32)


def pack_kernel(*refs):
    sources, (payload, *fields), held, sems = refs[:11], refs[11:14], refs[14:23], refs[23]
    copies = [pltpu.make_async_copy(a, b, sems.at[i]) for i, (a, b) in enumerate(zip(sources[:9], held))]
    pieces = (sems.shape[0] - 9) // 2
    step = fields[0].shape[0] // pieces
    slow = [
        pltpu.make_async_copy(
            a.at[pl.ds(k * step, step)], b.at[pl.ds(k * step, step)], sems.at[9 + n * pieces + k]
        )
        for n, (a, b) in enumerate(zip(sources[9:], fields))
        for k in range(pieces)
    ]
    for copy in copies + slow:
        copy.start()
    for copy in copies:
        copy.wait()
    residual, azimuth, elevation, brick, cell, force, px, py, pz = held
    cosine = jnp.cos(elevation[0])
    value = residual[0]
    gates, points = value.shape[1], px.shape[1]
    rest = jnp.zeros((1, gates - 2 * points), F32)
    rows = [
        cosine * jnp.cos(azimuth[0]) * value,
        cosine * jnp.sin(azimuth[0]) * value,
        jnp.sin(elevation[0]) * value,
        brick[...].astype(F32),
        cell[0].astype(F32),
        jnp.concatenate([force[0], force[1], force[2], px[...]], axis=1),
        jnp.concatenate([py[...], pz[...], rest], axis=1),
        jnp.zeros((1, gates), F32),
    ]
    for r, row in enumerate(rows):
        payload[r : r + 1, :] = row
    for copy in slow:
        copy.wait()


def edges(sides, size_x):
    if sides == 1:
        return [jnp.where(lax.axis_index("stream") == 0, size_x - HALO, 0)]
    return [size_x - HALO, 0]


def lines_of(payload, spans, start_x, size_y, size_z):
    brick = payload[3:4, :].astype(jnp.int32)
    cell = payload[4:5, :].astype(jnp.int32)
    away = brick - lax.axis_index("span")
    away = jnp.where(away < 0, away + spans, away)
    x = cell // (size_y * size_z)
    y = cell // size_z % size_y
    upper = (away == 1) & (y < HALO)
    lower = (away == spans - 1) & (y >= size_y - HALO)
    row = jnp.where(away == 0, y, jnp.where(upper, y + size_y, jnp.where(lower, y + 2 * HALO, -1)))
    return jnp.where(row < 0, -1, (x - start_x) * (size_y + 2 * HALO) + row), cell % size_z


def spread_points(payload_of, near, out, start_x, planes, size_y, size_z, first):
    ext_y = size_y + 2 * HALO
    height = planes * ext_y
    points = payload_of(0).shape[1] // 4
    count = len(near) * points
    rows = [[payload_of(j)[r : r + 1, :] for r in (5, 6)] for j, _ in near]

    def joined(r, k):
        return jnp.concatenate([pair[r][:, k * points : (k + 1) * points] for pair in rows], axis=1)

    px, pz = joined(0, 3), joined(1, 1)
    py = jnp.concatenate(
        [pair[1][:, 0:points] + F32(side * size_y) for pair, (_, side) in zip(rows, near)], axis=1
    )
    y_row = lax.broadcasted_iota(jnp.int32, (ext_y, count), 0)
    by = bump(jnp.where(y_row < size_y + HALO, y_row, y_row - ext_y).astype(F32) - py)
    x_cell = (lax.broadcasted_iota(jnp.int32, (planes, count), 0) + start_x).astype(F32)
    bx = bump(x_cell - px)
    z_cell = lax.broadcasted_iota(jnp.int32, (size_z, count), 0) + lax.axis_index("vert") * size_z
    bz_high, bz_low = two_parts(bump(z_cell.astype(F32) - pz))
    cross = jnp.concatenate([by * bx[x : x + 1] for x in range(planes)], axis=0)
    parts = [two_parts(cross * joined(0, c)) for c in range(3)]
    by_high = dot_lanes(jnp.concatenate([part for pair in parts for part in pair], axis=0), bz_high)
    by_low = dot_lanes(jnp.concatenate([high for high, _ in parts], axis=0), bz_low)
    for c in range(3):
        high = 2 * c * height
        both = by_high[high : high + height] + by_high[high + height : high + 2 * height]
        both += by_low[c * height : (c + 1) * height]
        out[c] = both if first is None else first[c] + both


def spread_gates(payload_of, spans, sources, out, start_x, planes, size_y, size_z, unroll=False):
    height = planes * (size_y + 2 * HALO)
    gates = payload_of(0).shape[1]
    row_id = lax.broadcasted_iota(jnp.int32, (height, gates), 0)
    z_id = lax.broadcasted_iota(jnp.int32, (size_z, gates), 0)

    def one_source(j, carry):
        one = payload_of(j)
        line, z = lines_of(one, spans, start_x, size_y, size_z)
        pick = jnp.where(row_id == line, 1.0, 0.0).astype(BF16)
        there = jnp.where(z_id == z, 1.0, 0.0).astype(BF16)
        high, low = zip(*[two_parts(one[c : c + 1, :]) for c in range(3)])
        if height <= 128:
            sums = dot_lanes(jnp.concatenate([pick * part for part in high + low], axis=0), there)
            for c in range(3):
                more = sums[(c + 3) * height : (c + 4) * height]
                out[c] += sums[c * height : (c + 1) * height] + more
            return carry
        scale = [256.0 / jnp.maximum(jnp.max(jnp.abs(part.astype(F32)), axis=1, keepdims=True), 1e-30) for part in low]
        low = [(pick * (part.astype(F32) * by).astype(BF16)).astype(F8) for part, by in zip(low, scale)]
        sums = dot_lanes(jnp.concatenate([pick * part for part in high], axis=0), there)
        rest = dot_lanes(jnp.concatenate(low, axis=0), there.astype(F8))
        for c in range(3):
            lines = slice(c * height, (c + 1) * height)
            out[c] += sums[lines] + rest[lines] * (1.0 / scale[c])
        return carry

    if unroll:
        for j in range(*sources):
            one_source(j, 0)
    else:
        lax.fori_loop(*sources, one_source, 0)


def near_of(spans):
    return ((0, 0), (spans - 1, -1), (2 if spans == 4 else 1, 1))


def first_kernel(spans, dims, payload, out):
    size_x, size_y, size_z = dims
    spread_points(lambda j: payload, near_of(spans)[:1], out, 0, size_x, size_y, size_z, None)
    spread_gates(lambda j: payload, spans, (0, 1), out, 0, size_x, size_y, size_z, unroll=True)


def payload_in(refs, j):
    return refs[0].at[j] if len(refs) == 1 else refs[j]


def second_kernel(spans, dims, count, *refs):
    payloads, (first, out) = refs[:count], refs[count:]
    for c in range(3):
        out[c] = first[c]
    spread_gates(lambda j: payload_in(payloads, j), spans, (1, spans), out, 0, *dims, unroll=count > 1)


def third_kernel(spans, dims, count, *refs):
    payloads, second, out = refs[:count], refs[count], refs[-1]
    spread_points(lambda j: payload_in(payloads, j), near_of(spans)[1:], out, 0, *dims, second)


def gather_kernel(spans, sides, count, *refs):
    payloads, (kappa, sigma), outs = refs[:count], refs[count : count + 2], refs[count + 2 :]
    size_x, size_y, size_z = kappa.shape
    for out, start in zip(outs, edges(sides, size_x)):
        each = payloads[0].shape[-1] // size_z
        for j in range(spans):
            one = payload_in(payloads, j)
            for part in range(each):
                out[j * each + part] = one[:, part * size_z : (part + 1) * size_z]
        for i in range(HALO):
            for k, field in enumerate((kappa, sigma)):
                plane = field[start + i]
                for part in range(size_y // 8):
                    out[spans * each + (2 * i + k) * (size_y // 8) + part] = plane[8 * part : 8 * part + 8]

def slab_kernel(kappa, sigma, to_upper, to_lower):
    size_y = kappa.shape[1]
    to_upper[:, 0:HALO] = kappa[:, size_y - HALO :]
    to_upper[:, HALO:] = sigma[:, size_y - HALO :]
    to_lower[:, 0:HALO] = kappa[:, 0:HALO]
    to_lower[:, HALO:] = sigma[:, 0:HALO]


def corner_kernel(sides, upper, lower, *outs):
    for out, start in zip(outs, edges(sides, upper.shape[0])):
        out[:, 0 : 2 * HALO] = upper[pl.ds(start, HALO)]
        out[:, 2 * HALO :] = lower[pl.ds(start, HALO)]


def strip_kernel(spans, sides, dims, *refs):
    size_x, size_y, size_z = dims
    starts = edges(sides, size_x)
    starts = [size_x - HALO - starts[0]] if sides == 1 else starts[::-1]
    for packed, strip, start in zip(refs[:sides], refs[sides:], starts):
        each = (packed.shape[0] - HALO * 2 * size_y // 8) // spans

        def payload_of(j, packed=packed, each=each):
            return jnp.concatenate([packed[j * each + part] for part in range(each)], axis=1)

        spread_points(payload_of, near_of(spans), strip, start, HALO, size_y, size_z, None)
        spread_gates(payload_of, spans, (0, spans), strip, start, HALO, size_y, size_z, unroll=spans == 4)


def extend_kernel(sides, *refs):
    own, kappa, sigma, upper, lower = refs[:5]
    strips, others, corners = (refs[5 + k * sides : 5 + (k + 1) * sides] for k in range(3))
    source, kappa_ext, face = refs[5 + 3 * sides :]
    size_x, size_y, size_z = kappa.shape
    ext_y = size_y + 2 * HALO
    for x in range(size_x + sides * HALO):
        if x < size_x:
            kappa_ext[x] = jnp.concatenate([kappa[x], upper[x, 0:HALO], lower[x, 0:HALO]], axis=0)
            sig = jnp.concatenate([sigma[x], upper[x, HALO:], lower[x, HALO:]], axis=0)
        else:
            packed, corner = others[(x - size_x) // HALO], corners[(x - size_x) // HALO]
            i = (x - size_x) % HALO
            tiles = size_y // 8
            base = packed.shape[0] - (HALO - i) * 2 * tiles
            slab = [packed[base + k] for k in range(2 * tiles)]
            up, low = corner[i, 0 : 2 * HALO], corner[i, 2 * HALO :]
            kappa_ext[x] = jnp.concatenate([*slab[:tiles], up[0:HALO], low[0:HALO]], axis=0)
            sig = jnp.concatenate([*slab[tiles:], up[HALO:], low[HALO:]], axis=0)
        for c in range(3):
            if x < size_x:
                value = own[c, x * ext_y : (x + 1) * ext_y, :]
            else:
                place = (x - size_x) % HALO * ext_y
                value = strips[(x - size_x) // HALO][c, place : place + ext_y, :]
            source[c, x] = value * sig
    planes, vert = kappa_ext.shape[0], lax.axis_index("vert")
    side = pl.ds(pl.multiple_of(jnp.where(vert == 0, size_z - 128, 0), 128), 128)
    fields = [[source[c, x, :, side] for x in range(planes)] for c in range(3)]
    fields.append([kappa_ext[x, :, side] for x in range(planes)])
    fields = jnp.concatenate([jnp.concatenate(field, axis=1) for field in fields], axis=0)
    lane = lax.broadcasted_iota(jnp.int32, (1, 128), 1)
    lane = (lane + vert + 127) & 127
    layer = jnp.where(vert == 0, 127 - lane // 32, lane // 32)
    place = lax.broadcasted_iota(jnp.int32, (planes * 128, 128), 0)
    pick = jnp.where(place == lane % 32 * 128 + layer, 1.0, 0.0).astype(BF16)
    high, rest = two_parts(fields)
    low = (fields - high.astype(F32) - rest.astype(F32)).astype(BF16)
    sums = jnp.dot(jnp.concatenate([high, rest, low], axis=0), pick, preferred_element_type=F32)
    for k in range(4):
        parts = [sums[(4 * part + k) * ext_y : (4 * part + k + 1) * ext_y] for part in range(3)]
        face[k] = parts[0] + (parts[1] + parts[2])


def lanes_on(values, step, lane, beyond=None):
    tiles = [values[:, k : k + 128] for k in range(0, values.shape[1], 128)]
    turned = [pltpu.roll(tile, step % 128, 1) for tile in tiles]
    edge = lane == (0 if step == 1 else 127)
    entering = turned[1:] + turned[:1] if step == -1 else turned[-1:] + turned[:-1]
    if beyond is not None:
        entering[-1 if step == -1 else 0] = beyond
    return jnp.concatenate([jnp.where(edge, new, tile) for new, tile in zip(entering, turned)], axis=1)


def each_plane(count, step, unroll=8):
    whole = count // unroll * unroll
    lax.fori_loop(0, whole, lambda i, carry: (step(i), carry)[1], 0, unroll=unroll)
    for i in range(whole, count):
        step(i)


def coefficient_kernel(sides, size_x, kappa_ext, root, ax, ay, aym, az, azm, keep):
    planes, ext_y, size_z = kappa_ext.shape
    stream, last = lax.axis_index("stream"), lax.axis_size("stream") - 1
    place = lax.broadcasted_iota(jnp.int32, (ext_y, size_z), 1)
    lane = lax.broadcasted_iota(jnp.int32, (ext_y, 128), 1)

    def roots(x):
        root[x] = jnp.sqrt(kappa_ext[x])

    each_plane(planes, roots)

    def faces(x):
        after = jnp.where(x == planes - 1, 0, x + 1)
        here = root[x]
        wall = ((x == planes - 1) & (stream == 0)) | ((x == size_x - 1) & (stream == last))
        ax[x] = here * root[after] * jnp.where(wall, 0.0, 1.0)
        up = here * pltpu.roll(here, ext_y - 1, 0)
        ay[x] = up
        aym[x] = pltpu.roll(up, 1, 0)
        up = jnp.where(place == size_z - 1, 0.0, here * lanes_on(here, -1, lane))
        az[x] = up
        azm[x] = lanes_on(up, 1, lane)

    each_plane(planes, faces)

    def rest(x):
        before = jnp.where(x == 0, planes - 1, x - 1)
        keep[x] = 1.0 - (ax[x] + ax[before] + ay[x] + aym[x] + az[x] + azm[x])

    each_plane(planes, rest)


def diffuse_kernel(sides, source, root, ax, ay, aym, az, azm, keep, sent, face, out, *scratch):
    ping, pong, halo, edge, az_all, azm_all, keep_all, done, sems = scratch
    planes, ext_y, size_z = root.shape
    size_x, size_y = done.shape[1], done.shape[2]
    stream, vert = lax.axis_index("stream"), lax.axis_index("vert")
    last = lax.axis_size("stream") - 1
    lane = lax.broadcasted_iota(jnp.int32, (ext_y, 128), 1)
    spot = (lane + 128 - vert) & 127
    plane, near = spot % 32, spot < 32

    def plane_on(values):
        return jnp.where(plane == planes - 1, pltpu.roll(values, planes - 1, 1), pltpu.roll(values, 127, 1))

    def plane_back(values):
        return jnp.where(plane == 0, pltpu.roll(values, 129 - planes, 1), pltpu.roll(values, 1, 1))

    here = jnp.sqrt(face[3])
    wall = ((plane == planes - 1) & (stream == 0)) | ((plane == size_x - 1) & (stream == last))
    ax_h = jnp.where(wall, 0.0, here * plane_on(here))
    axm_h = plane_back(ax_h)
    ay_h = here * pltpu.roll(here, ext_y - 1, 0)
    aym_h = pltpu.roll(ay_h, 1, 0)
    far_h = jnp.where(spot >= 96, 0.0, here * pltpu.roll(here, 96, 1))
    back = (2 * vert - 1) & 127
    joint = jnp.where(near, here * jnp.sqrt(pltpu.roll(sent[3], back, 1)), 0.0)
    near_h = jnp.where(near, joint, pltpu.roll(far_h, 32, 1))
    keep_h = 1.0 - (ax_h + axm_h + ay_h + aym_h + far_h + near_h)
    for c in range(3):
        halo[0, c] = face[c]
        edge[c] = pltpu.roll(sent[c], back, 1)

    above, below = (lane == 127) & (vert == 0), (lane == 0) & (vert == 1)

    for x in range(planes):
        beside = pltpu.roll(joint, 127 - x, 1)
        top, bottom = jnp.where(above, beside, 0.0), jnp.where(below, beside, 0.0)
        none = [jnp.zeros((ext_y, 128), F32)] * (size_z // 128 - 1)
        top, bottom = jnp.concatenate([*none, top], axis=1), jnp.concatenate([bottom, *none], axis=1)
        az_all[x] = az[x] + top
        azm_all[x] = azm[x] + bottom
        keep_all[x] = keep[x] - (top + bottom)

    side = pl.ds(pl.multiple_of(jnp.where(vert == 0, size_z - 128, 0), 128), 128)
    step, copies = size_x // sems.shape[0], []

    def one_pass(p, old, new):
        deep = PASSES - 1 - p
        now, later = p % 2, (p + 1) % 2
        if deep:
            for c in range(3):
                value = halo[now, c]
                moved = keep_h * value + ax_h * plane_on(value) + axm_h * plane_back(value)
                moved += ay_h * pltpu.roll(value, ext_y - 1, 0) + aym_h * pltpu.roll(value, 1, 0)
                moved += far_h * pltpu.roll(value, 96, 1)
                halo[later, c] = moved + near_h * jnp.where(near, edge[c], pltpu.roll(value, 32, 1))

        for x in range(planes if deep else size_x):
            after, before = (x + 1) % planes, (x - 1) % planes
            for c in range(3):
                value = old[c, x]
                beside = pltpu.roll(halo[now, c], 127 - x, 1)
                moved = keep_all[x] * value
                moved += ax[x] * old[c, after] + ax[before] * old[c, before]
                moved += ay[x] * pltpu.roll(value, ext_y - 1, 0) + aym[x] * pltpu.roll(value, 1, 0)
                moved += az_all[x] * lanes_on(value, -1, lane, beside) + azm_all[x] * lanes_on(value, 1, lane, beside)
                new[c, x] = moved if deep else moved[0:size_y]
            if not deep and (x + 1) % step == 0:
                part = pl.ds(x + 1 - step, step)
                copies.append(pltpu.make_async_copy(done.at[:, part], out.at[:, part], sems.at[x // step]))
                copies[-1].start()
        if deep > 1:
            for c in range(3):
                beside = pltpu.roll(new[c, 0, :, side], 1, 1)
                for x in range(1, planes):
                    beside = jnp.where(spot == x, pltpu.roll(new[c, x, :, side], x + 1, 1), beside)
                edge[c] = beside

    one_pass(0, source, pong)
    one_pass(1, pong, ping)
    one_pass(2, ping, pong)
    one_pass(3, pong, done)
    for copy in copies:
        copy.wait()


def call(kernel, outs, scratch, flops, *args, left=(), aliases=(), room=8, far=False):
    moved = sum(4 * a.size for a in args) + sum(4 * o.size for o in outs)
    spaces = [pltpu.HBM if i in left else pltpu.VMEM for i in range(len(args))]
    return pl.pallas_call(
        kernel,
        out_shape=outs,
        in_specs=[pl.BlockSpec(memory_space=space) for space in spaces],
        out_specs=[pl.BlockSpec(memory_space=pltpu.HBM if far else pltpu.VMEM)] * len(outs),
        scratch_shapes=scratch,
        input_output_aliases=dict(aliases),
        compiler_params=pltpu.CompilerParams(vmem_limit_bytes=room * 1024 * 1024),
        cost_estimate=pl.CostEstimate(flops=flops, bytes_accessed=moved, transcendentals=0),
    )(*args)


def ring(array, step):
    count = lax.axis_size("span")
    return lax.ppermute(array, "span", [(i, (i + step) % count) for i in range(count)])


def across_bands(arrays):
    count = lax.axis_size("stream")
    if count == 2:
        return [lax.ppermute(arrays[0], "stream", [(0, 1), (1, 0)])]
    return [
        lax.ppermute(arrays[1], "stream", [(i + 1, i) for i in range(count - 1)]),
        lax.ppermute(arrays[0], "stream", [(i, i + 1) for i in range(count - 1)]),
    ]


def on_device(
    kappa,
    sigma,
    gate_residual,
    gate_azimuth,
    gate_elevation,
    gate_brick,
    gate_cell,
    blade_force,
    point_x,
    point_y,
    point_z,
):
    size_x, size_y, size_z = kappa.shape
    spans = lax.axis_size("span")
    sides = 1 if lax.axis_size("stream") == 2 else 2
    gates = gate_residual.shape[2]
    ext_x, ext_y = size_x + sides * HALO, size_y + 2 * HALO
    shape = lambda *dims: jax.ShapeDtypeStruct(dims, F32)
    inputs = [
        gate_residual,
        gate_azimuth,
        gate_elevation,
        gate_brick.reshape(1, gates),
        gate_cell,
        blade_force,
        point_x,
        point_y,
        point_z,
        kappa,
        sigma,
    ]
    payload, kappa, sigma = call(
        pack_kernel,
        [shape(8, gates)] + [shape(size_x, size_y, size_z)] * 2,
        [pltpu.VMEM(a.shape, a.dtype) for a in inputs[:9]] + [pltpu.SemaphoreType.DMA((9 + 2 * 4,))],
        1000,
        *[pltpu.with_memory_space_constraint(a, pltpu.HBM) for a in inputs],
        left=range(len(inputs)),
    )
    if spans == 4:
        payloads = [payload, ring(payload, 2), ring(payload, -1), ring(payload, 1)]
    else:
        payloads = [jnp.roll(lax.all_gather(payload, "span"), -lax.axis_index("span"), axis=0)]
    dims = (size_x, size_y, size_z)
    work = 12 * size_x * ext_y * size_z * gates
    planes = shape(3, size_x * ext_y, size_z)
    (own,) = call(functools.partial(first_kernel, spans, dims), [planes], [], work, payload, room=24)
    parts = spans * gates // size_z + HALO * 2 * size_y // 8
    to_upper, to_lower = call(slab_kernel, [shape(size_x, 2 * HALO, size_z)] * 2, [], 1000, kappa, sigma)
    others = call(
        functools.partial(gather_kernel, spans, sides, len(payloads)),
        [shape(parts, 8, size_z)] * sides,
        [],
        1000,
        *payloads,
        kappa,
        sigma,
    )
    others = across_bands(others)
    from_lower, from_upper = ring(to_upper, 1), ring(to_lower, -1)
    (own,) = call(
        functools.partial(second_kernel, spans, dims, len(payloads)),
        [planes],
        [],
        work * (spans - 1),
        *payloads,
        own,
        aliases=((len(payloads), 0),),
        room=24,
    )
    corners = call(
        functools.partial(corner_kernel, sides),
        [shape(HALO, 4 * HALO, size_z)] * sides,
        [],
        1000,
        from_upper,
        from_lower,
    )
    (own,) = call(
        functools.partial(third_kernel, spans, dims, len(payloads)),
        [planes],
        [],
        work // 4,
        *payloads,
        own,
        *corners,
        aliases=((len(payloads), 0),),
        room=24,
    )
    corners = across_bands(corners)
    strips = call(
        functools.partial(strip_kernel, spans, sides, dims),
        [shape(3, HALO * ext_y, size_z)] * sides,
        [],
        work // 4 * spans,
        *others,
        room=24,
    )
    source, kappa_ext, face = call(
        functools.partial(extend_kernel, sides),
        [shape(3, ext_x, ext_y, size_z), shape(ext_x, ext_y, size_z), shape(4, ext_y, 128)],
        [],
        1000,
        own,
        kappa,
        sigma,
        from_upper,
        from_lower,
        *strips,
        *others,
        *corners,
    )
    other_face = lax.ppermute(face, "vert", [(0, 1), (1, 0)])
    main = (ext_x, ext_y, size_z)
    coefficients = call(
        functools.partial(coefficient_kernel, sides, size_x), [shape(*main)] * 7, [], 30 * ext_x * ext_y * size_z, kappa_ext
    )
    scratch = [(3, *main)] * 2 + [(2, 3, ext_y, 128), (3, ext_y, 128)] + [main] * 3 + [(3, size_x, size_y, size_z)]
    (field,) = call(
        functools.partial(diffuse_kernel, sides),
        [shape(3, size_x, size_y, size_z)],
        [pltpu.VMEM(dims, F32) for dims in scratch] + [pltpu.SemaphoreType.DMA((4,))],
        60 * 3 * ext_x * ext_y * size_z,
        source,
        *coefficients,
        face,
        other_face,
        room=20,
        far=True,
    )
    return field


def solution(mesh):
    placed = (
        P(("grp", "stream"), "span", "vert"),
        P(("grp", "stream"), "span", "vert"),
        P(("grp", "stream"), "vert", "span"),
        P(("grp", "stream"), "vert", "span"),
        P(("grp", "stream"), "vert", "span"),
        P(("grp", "stream"), "vert", "span", None),
        P(("grp", "stream"), "vert", "span"),
        P(None, ("grp", "stream"), "span"),
        P(("grp", "stream"), "span"),
        P(("grp", "stream"), "span"),
        P(("grp", "stream"), "span"),
    )
    return jax.shard_map(
        on_device,
        mesh=mesh,
        in_specs=placed,
        out_specs=P(None, ("grp", "stream"), "span", "vert"),
        check_vma=False,
    )
```

```python
import functools

import jax
import jax.numpy as jnp
from jax import lax
from jax.experimental import pallas as pl
from jax.experimental.pallas import tpu as pltpu
from jax.sharding import PartitionSpec as P

SPREAD = 6
PASSES = 4
HALO = 4
BF16 = jnp.bfloat16
F32 = jnp.float32
F8 = jnp.float8_e4m3fn
CONTRACT_LANES = (((1,), (1,)), ((), ()))


def bump(distance):
    scaled = distance * F32(1.0 / SPREAD)
    return jnp.square(jnp.maximum(0.0, 1.0 - scaled * scaled))


def two_parts(values):
    high = values.astype(BF16)
    return high, (values - high.astype(F32)).astype(BF16)


def dot_lanes(left, right):
    return lax.dot_general(left, right, CONTRACT_LANES, preferred_element_type=F32)


def pack_kernel(*refs):
    sources, (payload, *fields), held, sems = refs[:11], refs[11:14], refs[14:23], refs[23]
    copies = [pltpu.make_async_copy(a, b, sems.at[i]) for i, (a, b) in enumerate(zip(sources[:9], held))]
    pieces = (sems.shape[0] - 9) // 2
    step = fields[0].shape[0] // pieces
    slow = [
        pltpu.make_async_copy(
            a.at[pl.ds(k * step, step)], b.at[pl.ds(k * step, step)], sems.at[9 + n * pieces + k]
        )
        for n, (a, b) in enumerate(zip(sources[9:], fields))
        for k in range(pieces)
    ]
    for copy in copies + slow:
        copy.start()
    for copy in copies:
        copy.wait()
    residual, azimuth, elevation, brick, cell, force, px, py, pz = held
    cosine = jnp.cos(elevation[0])
    value = residual[0]
    gates, points = value.shape[1], px.shape[1]
    rest = jnp.zeros((1, gates - 2 * points), F32)
    rows = [
        cosine * jnp.cos(azimuth[0]) * value,
        cosine * jnp.sin(azimuth[0]) * value,
        jnp.sin(elevation[0]) * value,
        brick[...].astype(F32),
        cell[0].astype(F32),
        jnp.concatenate([force[0], force[1], force[2], px[...]], axis=1),
        jnp.concatenate([py[...], pz[...], rest], axis=1),
        jnp.zeros((1, gates), F32),
    ]
    for r, row in enumerate(rows):
        payload[r : r + 1, :] = row
    for copy in slow:
        copy.wait()


def edges(sides, size_x):
    if sides == 1:
        return [jnp.where(lax.axis_index("stream") == 0, size_x - HALO, 0)]
    return [size_x - HALO, 0]


def lines_of(payload, spans, start_x, size_y, size_z):
    brick = payload[3:4, :].astype(jnp.int32)
    cell = payload[4:5, :].astype(jnp.int32)
    away = brick - lax.axis_index("span")
    away = jnp.where(away < 0, away + spans, away)
    x = cell // (size_y * size_z)
    y = cell // size_z % size_y
    upper = (away == 1) & (y < HALO)
    lower = (away == spans - 1) & (y >= size_y - HALO)
    row = jnp.where(away == 0, y, jnp.where(upper, y + size_y, jnp.where(lower, y + 2 * HALO, -1)))
    return jnp.where(row < 0, -1, (x - start_x) * (size_y + 2 * HALO) + row), cell % size_z


def spread_points(payload_of, near, out, start_x, planes, size_y, size_z, first):
    ext_y = size_y + 2 * HALO
    points = payload_of(0).shape[1] // 4
    y_row = lax.broadcasted_iota(jnp.int32, (ext_y, points), 0)
    y_cell = jnp.where(y_row < size_y + HALO, y_row, y_row - ext_y).astype(F32)
    x_cell = (lax.broadcasted_iota(jnp.int32, (planes, points), 0) + start_x).astype(F32)
    z_cell = lax.broadcasted_iota(jnp.int32, (size_z, points), 0) + lax.axis_index("vert") * size_z
    z_cell = z_cell.astype(F32)
    written = set()
    for j, side in near:
        upper, lower = (payload_of(j)[r : r + 1, :] for r in (5, 6))
        force = [upper[:, c * points : (c + 1) * points] for c in range(3)]
        py = lower[:, 0:points] + F32(side * size_y)
        bx, by = bump(x_cell - upper[:, 3 * points :]), bump(y_cell - py)
        bz_high, bz_low = two_parts(bump(z_cell - lower[:, points : 2 * points]))
        tiles = [t for t in range(0, ext_y, 8) if t >= size_y or side == 0 or t == (0 if side < 0 else size_y - 8)]
        by = jnp.concatenate([by[t : t + 8] for t in tiles], axis=0)
        cross = jnp.concatenate([by * bx[x : x + 1] for x in range(planes)], axis=0)
        parts = [two_parts(cross * force[c]) for c in range(3)]
        by_high = dot_lanes(jnp.concatenate([part for pair in parts for part in pair], axis=0), bz_high)
        by_low = dot_lanes(jnp.concatenate([high for high, _ in parts], axis=0), bz_low)
        height = cross.shape[0]
        for c in range(3):
            high = 2 * c * height
            both = by_high[high : high + height] + by_high[high + height : high + 2 * height]
            both += by_low[c * height : (c + 1) * height]
            for x in range(planes):
                for k, t in enumerate(tiles):
                    rows = slice(x * ext_y + t, x * ext_y + t + 8)
                    place = (x * len(tiles) + k) * 8
                    value = both[place : place + 8]
                    before = out if t in written else first
                    out[c, rows, :] = value if before is None else before[c, rows, :] + value
        written.update(tiles)


def spread_gates(payload_of, spans, sources, out, start_x, planes, size_y, size_z, unroll=False):
    height = planes * (size_y + 2 * HALO)
    gates = payload_of(0).shape[1]
    row_id = lax.broadcasted_iota(jnp.int32, (height, gates), 0)
    z_id = lax.broadcasted_iota(jnp.int32, (size_z, gates), 0)

    def one_source(j, carry):
        one = payload_of(j)
        line, z = lines_of(one, spans, start_x, size_y, size_z)
        pick = jnp.where(row_id == line, 1.0, 0.0).astype(BF16)
        there = jnp.where(z_id == z, 1.0, 0.0).astype(BF16)
        high, low = zip(*[two_parts(one[c : c + 1, :]) for c in range(3)])
        if height <= 128:
            sums = dot_lanes(jnp.concatenate([pick * part for part in high + low], axis=0), there)
            for c in range(3):
                more = sums[(c + 3) * height : (c + 4) * height]
                out[c] += sums[c * height : (c + 1) * height] + more
            return carry
        scale = [256.0 / jnp.maximum(jnp.max(jnp.abs(part.astype(F32)), axis=1, keepdims=True), 1e-30) for part in low]
        low = [(pick * (part.astype(F32) * by).astype(BF16)).astype(F8) for part, by in zip(low, scale)]
        sums = dot_lanes(jnp.concatenate([pick * part for part in high], axis=0), there)
        rest = dot_lanes(jnp.concatenate(low, axis=0), there.astype(F8))
        for c in range(3):
            lines = slice(c * height, (c + 1) * height)
            out[c] += sums[lines] + rest[lines] * (1.0 / scale[c])
        return carry

    if unroll:
        for j in range(*sources):
            one_source(j, 0)
    else:
        lax.fori_loop(*sources, one_source, 0)


def near_of(spans):
    return ((0, 0), (spans - 1, -1), (2 if spans == 4 else 1, 1))


def first_kernel(spans, dims, payload, out):
    size_x, size_y, size_z = dims
    spread_points(lambda j: payload, near_of(spans)[:1], out, 0, size_x, size_y, size_z, None)
    spread_gates(lambda j: payload, spans, (0, 1), out, 0, size_x, size_y, size_z, unroll=True)


def payload_in(refs, j):
    return refs[0].at[j] if len(refs) == 1 else refs[j]


def second_kernel(spans, dims, count, *refs):
    payloads, (first, out) = refs[:count], refs[count:]
    for c in range(3):
        out[c] = first[c]
    spread_gates(lambda j: payload_in(payloads, j), spans, (1, spans), out, 0, *dims, unroll=count > 1)


def third_kernel(spans, dims, count, *refs):
    payloads, second, out = refs[:count], refs[count], refs[-1]
    spread_points(lambda j: payload_in(payloads, j), near_of(spans)[1:], out, 0, *dims, second)


def gather_kernel(spans, sides, count, *refs):
    payloads, (kappa, sigma), outs = refs[:count], refs[count : count + 2], refs[count + 2 :]
    size_x, size_y, size_z = kappa.shape
    for out, start in zip(outs, edges(sides, size_x)):
        each = payloads[0].shape[-1] // size_z
        for j in range(spans):
            one = payload_in(payloads, j)
            for part in range(each):
                out[j * each + part] = one[:, part * size_z : (part + 1) * size_z]
        for i in range(HALO):
            for k, field in enumerate((kappa, sigma)):
                plane = field[start + i]
                for part in range(size_y // 8):
                    out[spans * each + (2 * i + k) * (size_y // 8) + part] = plane[8 * part : 8 * part + 8]

def slab_kernel(kappa, sigma, to_upper, to_lower):
    size_y = kappa.shape[1]
    to_upper[:, 0:HALO] = kappa[:, size_y - HALO :]
    to_upper[:, HALO:] = sigma[:, size_y - HALO :]
    to_lower[:, 0:HALO] = kappa[:, 0:HALO]
    to_lower[:, HALO:] = sigma[:, 0:HALO]


def corner_kernel(sides, upper, lower, *outs):
    for out, start in zip(outs, edges(sides, upper.shape[0])):
        out[:, 0 : 2 * HALO] = upper[pl.ds(start, HALO)]
        out[:, 2 * HALO :] = lower[pl.ds(start, HALO)]


def strip_kernel(spans, sides, dims, *refs):
    size_x, size_y, size_z = dims
    starts = edges(sides, size_x)
    starts = [size_x - HALO - starts[0]] if sides == 1 else starts[::-1]
    for packed, strip, start in zip(refs[:sides], refs[sides:], starts):
        each = (packed.shape[0] - HALO * 2 * size_y // 8) // spans

        def payload_of(j, packed=packed, each=each):
            return jnp.concatenate([packed[j * each + part] for part in range(each)], axis=1)

        spread_points(payload_of, near_of(spans), strip, start, HALO, size_y, size_z, None)
        spread_gates(payload_of, spans, (0, spans), strip, start, HALO, size_y, size_z, unroll=spans == 4)


def extend_kernel(sides, *refs):
    own, kappa, sigma, upper, lower = refs[:5]
    strips, others, corners = (refs[5 + k * sides : 5 + (k + 1) * sides] for k in range(3))
    source, kappa_ext, face = refs[5 + 3 * sides :]
    size_x, size_y, size_z = kappa.shape
    ext_y = size_y + 2 * HALO
    for x in range(size_x + sides * HALO):
        if x < size_x:
            kappa_ext[x] = jnp.concatenate([kappa[x], upper[x, 0:HALO], lower[x, 0:HALO]], axis=0)
            sig = jnp.concatenate([sigma[x], upper[x, HALO:], lower[x, HALO:]], axis=0)
        else:
            packed, corner = others[(x - size_x) // HALO], corners[(x - size_x) // HALO]
            i = (x - size_x) % HALO
            tiles = size_y // 8
            base = packed.shape[0] - (HALO - i) * 2 * tiles
            slab = [packed[base + k] for k in range(2 * tiles)]
            up, low = corner[i, 0 : 2 * HALO], corner[i, 2 * HALO :]
            kappa_ext[x] = jnp.concatenate([*slab[:tiles], up[0:HALO], low[0:HALO]], axis=0)
            sig = jnp.concatenate([*slab[tiles:], up[HALO:], low[HALO:]], axis=0)
        for c in range(3):
            if x < size_x:
                value = own[c, x * ext_y : (x + 1) * ext_y, :]
            else:
                place = (x - size_x) % HALO * ext_y
                value = strips[(x - size_x) // HALO][c, place : place + ext_y, :]
            source[c, x] = value * sig
    planes, vert = kappa_ext.shape[0], lax.axis_index("vert")
    side = pl.ds(pl.multiple_of(jnp.where(vert == 0, size_z - 128, 0), 128), 128)
    fields = [[source[c, x, :, side] for x in range(planes)] for c in range(3)]
    fields.append([kappa_ext[x, :, side] for x in range(planes)])
    fields = jnp.concatenate([jnp.concatenate(field, axis=1) for field in fields], axis=0)
    lane = lax.broadcasted_iota(jnp.int32, (1, 128), 1)
    lane = (lane + vert + 127) & 127
    layer = jnp.where(vert == 0, 127 - lane // 32, lane // 32)
    place = lax.broadcasted_iota(jnp.int32, (planes * 128, 128), 0)
    pick = jnp.where(place == lane % 32 * 128 + layer, 1.0, 0.0).astype(BF16)
    high, rest = two_parts(fields)
    sums = jnp.dot(jnp.concatenate([high, rest], axis=0), pick, preferred_element_type=F32)
    for k in range(4):
        face[k] = sums[k * ext_y : (k + 1) * ext_y] + sums[(4 + k) * ext_y : (5 + k) * ext_y]


def lanes_on(values, step, lane, beyond=None):
    tiles = [values[:, k : k + 128] for k in range(0, values.shape[1], 128)]
    turned = [pltpu.roll(tile, step % 128, 1) for tile in tiles]
    edge = lane == (0 if step == 1 else 127)
    entering = turned[1:] + turned[:1] if step == -1 else turned[-1:] + turned[:-1]
    if beyond is not None:
        entering[-1 if step == -1 else 0] = beyond
    return jnp.concatenate([jnp.where(edge, new, tile) for new, tile in zip(entering, turned)], axis=1)


def each_plane(count, step, unroll=8):
    whole = count // unroll * unroll
    lax.fori_loop(0, whole, lambda i, carry: (step(i), carry)[1], 0, unroll=unroll)
    for i in range(whole, count):
        step(i)


def coefficient_kernel(sides, size_x, kappa_ext, root, ax, ay, aym, az, azm, keep):
    planes, ext_y, size_z = kappa_ext.shape
    stream, last = lax.axis_index("stream"), lax.axis_size("stream") - 1
    place = lax.broadcasted_iota(jnp.int32, (ext_y, size_z), 1)
    lane = lax.broadcasted_iota(jnp.int32, (ext_y, 128), 1)

    def roots(x):
        root[x] = jnp.sqrt(kappa_ext[x])

    each_plane(planes, roots)

    def faces(x):
        after = jnp.where(x == planes - 1, 0, x + 1)
        here = root[x]
        wall = ((x == planes - 1) & (stream == 0)) | ((x == size_x - 1) & (stream == last))
        ax[x] = here * root[after] * jnp.where(wall, 0.0, 1.0)
        up = here * pltpu.roll(here, ext_y - 1, 0)
        ay[x] = up
        aym[x] = pltpu.roll(up, 1, 0)
        up = jnp.where(place == size_z - 1, 0.0, here * lanes_on(here, -1, lane))
        az[x] = up
        azm[x] = lanes_on(up, 1, lane)

    each_plane(planes, faces)

    def rest(x):
        before = jnp.where(x == 0, planes - 1, x - 1)
        keep[x] = 1.0 - (ax[x] + ax[before] + ay[x] + aym[x] + az[x] + azm[x])

    each_plane(planes, rest)


def diffuse_kernel(sides, source, root, ax, ay, aym, az, azm, keep, sent, face, out, *scratch):
    ping, pong, halo, edge, az_all, azm_all, keep_all, done, sems = scratch
    planes, ext_y, size_z = root.shape
    size_x, size_y = done.shape[1], done.shape[2]
    stream, vert = lax.axis_index("stream"), lax.axis_index("vert")
    last = lax.axis_size("stream") - 1
    lane = lax.broadcasted_iota(jnp.int32, (ext_y, 128), 1)
    spot = (lane + 128 - vert) & 127
    plane, near = spot % 32, spot < 32

    def plane_on(values):
        return jnp.where(plane == planes - 1, pltpu.roll(values, planes - 1, 1), pltpu.roll(values, 127, 1))

    def plane_back(values):
        return jnp.where(plane == 0, pltpu.roll(values, 129 - planes, 1), pltpu.roll(values, 1, 1))

    here = jnp.sqrt(face[3])
    wall = ((plane == planes - 1) & (stream == 0)) | ((plane == size_x - 1) & (stream == last))
    ax_h = jnp.where(wall, 0.0, here * plane_on(here))
    axm_h = plane_back(ax_h)
    ay_h = here * pltpu.roll(here, ext_y - 1, 0)
    aym_h = pltpu.roll(ay_h, 1, 0)
    far_h = jnp.where(spot >= 96, 0.0, here * pltpu.roll(here, 96, 1))
    back = (2 * vert - 1) & 127
    joint = jnp.where(near, here * jnp.sqrt(pltpu.roll(sent[3], back, 1)), 0.0)
    near_h = jnp.where(near, joint, pltpu.roll(far_h, 32, 1))
    keep_h = 1.0 - (ax_h + axm_h + ay_h + aym_h + far_h + near_h)
    for c in range(3):
        halo[0, c] = face[c]
        edge[c] = pltpu.roll(sent[c], back, 1)

    above, below = (lane == 127) & (vert == 0), (lane == 0) & (vert == 1)

    for x in range(planes):
        beside = pltpu.roll(joint, 127 - x, 1)
        top, bottom = jnp.where(above, beside, 0.0), jnp.where(below, beside, 0.0)
        none = [jnp.zeros((ext_y, 128), F32)] * (size_z // 128 - 1)
        top, bottom = jnp.concatenate([*none, top], axis=1), jnp.concatenate([bottom, *none], axis=1)
        az_all[x] = az[x] + top
        azm_all[x] = azm[x] + bottom
        keep_all[x] = keep[x] - (top + bottom)

    side = pl.ds(pl.multiple_of(jnp.where(vert == 0, size_z - 128, 0), 128), 128)
    step, copies = size_x // sems.shape[0], []

    def one_pass(p, old, new):
        deep = PASSES - 1 - p
        now, later = p % 2, (p + 1) % 2
        if deep:
            for c in range(3):
                value = halo[now, c]
                moved = keep_h * value + ax_h * plane_on(value) + axm_h * plane_back(value)
                moved += ay_h * pltpu.roll(value, ext_y - 1, 0) + aym_h * pltpu.roll(value, 1, 0)
                moved += far_h * pltpu.roll(value, 96, 1)
                halo[later, c] = moved + near_h * jnp.where(near, edge[c], pltpu.roll(value, 32, 1))

        for x in range(planes if deep else size_x):
            after, before = (x + 1) % planes, (x - 1) % planes
            for c in range(3):
                value = old[c, x]
                beside = pltpu.roll(halo[now, c], 127 - x, 1)
                moved = keep_all[x] * value
                moved += ax[x] * old[c, after] + ax[before] * old[c, before]
                moved += ay[x] * pltpu.roll(value, ext_y - 1, 0) + aym[x] * pltpu.roll(value, 1, 0)
                moved += az_all[x] * lanes_on(value, -1, lane, beside) + azm_all[x] * lanes_on(value, 1, lane, beside)
                new[c, x] = moved if deep else moved[0:size_y]
            if not deep and (x + 1) % step == 0:
                part = pl.ds(x + 1 - step, step)
                copies.append(pltpu.make_async_copy(done.at[:, part], out.at[:, part], sems.at[x // step]))
                copies[-1].start()
        if deep > 1:
            for c in range(3):
                beside = pltpu.roll(new[c, 0, :, side], 1, 1)
                for x in range(1, planes):
                    beside = jnp.where(spot == x, pltpu.roll(new[c, x, :, side], x + 1, 1), beside)
                edge[c] = beside

    one_pass(0, source, pong)
    one_pass(1, pong, ping)
    one_pass(2, ping, pong)
    one_pass(3, pong, done)
    for copy in copies:
        copy.wait()


def call(kernel, outs, scratch, flops, *args, left=(), aliases=(), room=8, far=False):
    moved = sum(4 * a.size for a in args) + sum(4 * o.size for o in outs)
    spaces = [pltpu.HBM if i in left else pltpu.VMEM for i in range(len(args))]
    return pl.pallas_call(
        kernel,
        out_shape=outs,
        in_specs=[pl.BlockSpec(memory_space=space) for space in spaces],
        out_specs=[pl.BlockSpec(memory_space=pltpu.HBM if far else pltpu.VMEM)] * len(outs),
        scratch_shapes=scratch,
        input_output_aliases=dict(aliases),
        compiler_params=pltpu.CompilerParams(vmem_limit_bytes=room * 1024 * 1024),
        cost_estimate=pl.CostEstimate(flops=flops, bytes_accessed=moved, transcendentals=0),
    )(*args)


def ring(array, step):
    count = lax.axis_size("span")
    return lax.ppermute(array, "span", [(i, (i + step) % count) for i in range(count)])


def across_bands(arrays):
    count = lax.axis_size("stream")
    if count == 2:
        return [lax.ppermute(arrays[0], "stream", [(0, 1), (1, 0)])]
    return [
        lax.ppermute(arrays[1], "stream", [(i + 1, i) for i in range(count - 1)]),
        lax.ppermute(arrays[0], "stream", [(i, i + 1) for i in range(count - 1)]),
    ]


def on_device(
    kappa,
    sigma,
    gate_residual,
    gate_azimuth,
    gate_elevation,
    gate_brick,
    gate_cell,
    blade_force,
    point_x,
    point_y,
    point_z,
):
    size_x, size_y, size_z = kappa.shape
    spans = lax.axis_size("span")
    sides = 1 if lax.axis_size("stream") == 2 else 2
    gates = gate_residual.shape[2]
    ext_x, ext_y = size_x + sides * HALO, size_y + 2 * HALO
    shape = lambda *dims: jax.ShapeDtypeStruct(dims, F32)
    inputs = [
        gate_residual,
        gate_azimuth,
        gate_elevation,
        gate_brick.reshape(1, gates),
        gate_cell,
        blade_force,
        point_x,
        point_y,
        point_z,
        kappa,
        sigma,
    ]
    payload, kappa, sigma = call(
        pack_kernel,
        [shape(8, gates)] + [shape(size_x, size_y, size_z)] * 2,
        [pltpu.VMEM(a.shape, a.dtype) for a in inputs[:9]] + [pltpu.SemaphoreType.DMA((9 + 2 * 4,))],
        1000,
        *[pltpu.with_memory_space_constraint(a, pltpu.HBM) for a in inputs],
        left=range(len(inputs)),
    )
    if spans == 4:
        payloads = [payload, ring(payload, 2), ring(payload, -1), ring(payload, 1)]
    else:
        payloads = [jnp.roll(lax.all_gather(payload, "span"), -lax.axis_index("span"), axis=0)]
    dims = (size_x, size_y, size_z)
    work = 12 * size_x * ext_y * size_z * gates
    planes = shape(3, size_x * ext_y, size_z)
    (own,) = call(functools.partial(first_kernel, spans, dims), [planes], [], work, payload, room=24)
    parts = spans * gates // size_z + HALO * 2 * size_y // 8
    to_upper, to_lower = call(slab_kernel, [shape(size_x, 2 * HALO, size_z)] * 2, [], 1000, kappa, sigma)
    others = call(
        functools.partial(gather_kernel, spans, sides, len(payloads)),
        [shape(parts, 8, size_z)] * sides,
        [],
        1000,
        *payloads,
        kappa,
        sigma,
    )
    others = across_bands(others)
    from_lower, from_upper = ring(to_upper, 1), ring(to_lower, -1)
    (own,) = call(
        functools.partial(second_kernel, spans, dims, len(payloads)),
        [planes],
        [],
        work * (spans - 1),
        *payloads,
        own,
        aliases=((len(payloads), 0),),
        room=24,
    )
    corners = call(
        functools.partial(corner_kernel, sides),
        [shape(HALO, 4 * HALO, size_z)] * sides,
        [],
        1000,
        from_upper,
        from_lower,
    )
    (own,) = call(
        functools.partial(third_kernel, spans, dims, len(payloads)),
        [planes],
        [],
        work // 4,
        *payloads,
        own,
        *corners,
        aliases=((len(payloads), 0),),
        room=24,
    )
    corners = across_bands(corners)
    strips = call(
        functools.partial(strip_kernel, spans, sides, dims),
        [shape(3, HALO * ext_y, size_z)] * sides,
        [],
        work // 4 * spans,
        *others,
        room=24,
    )
    source, kappa_ext, face = call(
        functools.partial(extend_kernel, sides),
        [shape(3, ext_x, ext_y, size_z), shape(ext_x, ext_y, size_z), shape(4, ext_y, 128)],
        [],
        1000,
        own,
        kappa,
        sigma,
        from_upper,
        from_lower,
        *strips,
        *others,
        *corners,
    )
    other_face = lax.ppermute(face, "vert", [(0, 1), (1, 0)])
    main = (ext_x, ext_y, size_z)
    coefficients = call(
        functools.partial(coefficient_kernel, sides, size_x), [shape(*main)] * 7, [], 30 * ext_x * ext_y * size_z, kappa_ext
    )
    scratch = [(3, *main)] * 2 + [(2, 3, ext_y, 128), (3, ext_y, 128)] + [main] * 3 + [(3, size_x, size_y, size_z)]
    (field,) = call(
        functools.partial(diffuse_kernel, sides),
        [shape(3, size_x, size_y, size_z)],
        [pltpu.VMEM(dims, F32) for dims in scratch] + [pltpu.SemaphoreType.DMA((4,))],
        60 * 3 * ext_x * ext_y * size_z,
        source,
        *coefficients,
        face,
        other_face,
        room=20,
        far=True,
    )
    return field


def solution(mesh):
    placed = (
        P(("grp", "stream"), "span", "vert"),
        P(("grp", "stream"), "span", "vert"),
        P(("grp", "stream"), "vert", "span"),
        P(("grp", "stream"), "vert", "span"),
        P(("grp", "stream"), "vert", "span"),
        P(("grp", "stream"), "vert", "span", None),
        P(("grp", "stream"), "vert", "span"),
        P(None, ("grp", "stream"), "span"),
        P(("grp", "stream"), "span"),
        P(("grp", "stream"), "span"),
        P(("grp", "stream"), "span"),
    )
    return jax.shard_map(
        on_device,
        mesh=mesh,
        in_specs=placed,
        out_specs=P(None, ("grp", "stream"), "span", "vert"),
        check_vma=False,
    )
```
